32 devices in a mesh: own: 4 (over z), col: 2 (over x), mlp: 4 (over y, core).
Axes of the slice: x: 2, y: 2, z: 4, core: 2. Of those that a mesh axis runs over, the one named last changes fastest.
Arguments:
- features: bfloat16 [32768, 512], P(('own', 'col')), may hold values from -6 to 6
- nbr_page: int32 [1024, 32], P(('own', 'col')), may hold values from 0 to 32767, as said below
- nbr_weight: bfloat16 [1024, 32], P(('own', 'col')), may hold values from 0.0049743652 to 0.29882812
- labels: int32 [1024], P(('own', 'col')), may hold values from 0 to 255
- w_one: bfloat16 [512, 2048], P(None, 'mlp'), may hold values from -0.25 to 0.25
- w_two: bfloat16 [2048, 256], P('mlp'), may hold values from -0.125 to 0.125
Outputs:
- grad_one: float32 [512, 2048], P(None, 'mlp')
- grad_two: float32 [2048, 256], P('mlp')
The draws below stay inside these ranges and needn't reach their ends.
Inputs may be any that keep to these rules, and one draw needn't show every extreme that they name: `nbr_page`: page p is held by owner p // 4096 (owners numbered along own then col) at its row p % 4096. The 32 neighbours of a target are distinct pages listed in non-decreasing order of owner. Of the 4096 neighbour entries of the targets of one index of own and col, at most 1024 fall on one owner; one owner receives exactly 1024 entries from every index, and some owners receive none from some indices.
All inputs are finite; a program needn't handle non-finite values.
Results may differ from the reference program's by a relative error of at most 0.011.
Values may be sent and summed in bfloat16 or wider, within the bound.
A program may use at most 128 MiB of HBM per device.

```python
import math
import jax
import jax.numpy as jnp
from jax import lax

F = 512
H = 2048
C = 256
K = 32
TGT_DEV = 128
ROWS_DEV = 4096
OWNERS = 8
PAGES = 32768
TARGETS = 1024
MEAN_LOAD = 512


STRIDES = (10007, 10009, 10037, 10039, 10061, 10067, 10069, 10079)


def draw_nbr_page(key, part):
    entries = TGT_DEV * K
    hot_key, order_key, offset_key, stride_key, mixing_key = jax.random.split(key, 5)
    hottest = jax.random.randint(hot_key, (), 0, OWNERS).astype(jnp.int32)

    def one_block(block_id):
        others = jax.random.permutation(jax.random.fold_in(order_key, block_id), OWNERS - 1).astype(jnp.int32)
        others = others + (others >= hottest).astype(jnp.int32)
        sequence = jnp.concatenate([hottest[None], others])
        rank_load = jnp.full((OWNERS,), MEAN_LOAD, jnp.int32)
        rank_load = rank_load.at[0].set(2 * MEAN_LOAD).at[1].set(0)
        rank_load = rank_load.at[2].set(MEAN_LOAD + MEAN_LOAD // 2).at[3].set(MEAN_LOAD // 2)
        owner_load = jnp.zeros((OWNERS,), jnp.int32).at[sequence].set(rank_load)
        load_end = jnp.cumsum(owner_load).astype(jnp.int32)
        starts = load_end - owner_load
        entry_ids = jnp.arange(entries, dtype=jnp.int32)
        owner_ids = jnp.searchsorted(load_end, entry_ids, side='right').astype(jnp.int32)
        within = entry_ids - starts[owner_ids]
        offset = jax.random.randint(jax.random.fold_in(offset_key, block_id), (OWNERS,), 0, ROWS_DEV).astype(jnp.int32)
        chosen = jax.random.randint(jax.random.fold_in(stride_key, block_id), (OWNERS,), 0, 8)
        stride = jnp.asarray(STRIDES, jnp.int32)[chosen]
        local_row = (offset[owner_ids] + within * stride[owner_ids]) % ROWS_DEV
        flat_pages = (owner_ids * ROWS_DEV + local_row).astype(jnp.int32)
        mixing = jax.random.permutation(jax.random.fold_in(mixing_key, block_id), entries).astype(jnp.int32)
        mixed = flat_pages[mixing].reshape(TGT_DEV, K)
        return jnp.sort(mixed, axis=1).astype(jnp.int32)
    page_ids = lax.map(one_block, jnp.arange(OWNERS, dtype=jnp.int32))
    return page_ids.reshape(TARGETS, K).astype(jnp.int32)


def with_ends(drawn, stream_key, low, top_value):
    longest = drawn.shape.index(max(drawn.shape))
    spots = []
    for shift in (0, 1):
        where = [jax.random.randint(jax.random.fold_in(stream_key, axis), (), 0, length) for axis, length in enumerate(drawn.shape)]
        where[longest] = (where[longest] + shift) % drawn.shape[longest]
        spots.append(tuple(where))
    return drawn.at[spots[0]].set(low).at[spots[1]].set(top_value)


def block_levels(key, shape, cuts, low, high):
    loudness = 1.0
    for axis_at, shards_of in cuts:
        draws = jax.random.uniform(jax.random.fold_in(jax.random.fold_in(key, 6), axis_at), (shards_of,), jnp.float32, low / len(cuts), high / len(cuts))
        loudness = loudness * jnp.repeat(jnp.exp(draws), shape[axis_at] // shards_of).reshape((-1,) + (1,) * (len(shape) - 1 - axis_at))
    return loudness


def gaussian(own_key, shape, scale, bound, cuts=(), kind=jnp.bfloat16):
    loudness = block_levels(own_key, shape, cuts, -0.22, 0.18) if cuts else 1.0
    array = jax.random.normal(own_key, shape, jnp.float32) * scale * loudness
    return jnp.minimum(jnp.maximum(array, -bound), bound).astype(kind)


def setup_inputs(seed: int = 0) -> dict:
    key_list = jax.random.split(jax.random.key(seed), 7)
    return {
        "features": gaussian(key_list[0], (PAGES, F), 1.0, 6.0, ((0, 8),)),
        "nbr_page": draw_nbr_page(jax.random.fold_in(key_list[6], 71), 0),
        "nbr_weight": jnp.clip(jnp.exp(math.log(0.29882812) - 4.095571 * jax.random.uniform(key_list[2], (TARGETS, K), jnp.float32) ** block_levels(key_list[2], (TARGETS, K), ((0, 8),), -0.2, 0.2)), 0.0049743652, 0.29882812).astype(jnp.bfloat16),
        "labels": with_ends(jax.random.randint(key_list[3], (TARGETS,), 0, C), jax.random.fold_in(key_list[3], 1), 0, C - 1).astype(jnp.int32),
        "w_one": gaussian(key_list[4], (F, H), F ** -0.5, 0.25, ((1, 4),)),
        "w_two": gaussian(key_list[5], (H, C), H ** -0.5, 0.125, ((0, 4),)),
    }


def reference(features, nbr_page, nbr_weight, labels, w_one, w_two):
    pages_in = nbr_page.reshape(OWNERS, TGT_DEV, K)
    weights_in = nbr_weight.reshape(OWNERS, TGT_DEV, K)
    labels_in = labels.reshape(OWNERS, TGT_DEV)

    def one_block(totals, block_in):
        page_ids, weight_in, label_ids = block_in
        row_feats = features[page_ids.reshape(-1)]
        pre_act = jnp.dot(row_feats, w_one, preferred_element_type=jnp.float32)
        active = jnp.maximum(pre_act, 0.0).astype(jnp.bfloat16)
        hidden = jnp.einsum("tk,tkh->th", weight_in.astype(jnp.float32),
                            active.reshape(TGT_DEV, K, H).astype(jnp.float32)).astype(jnp.bfloat16)
        logits = jnp.dot(hidden, w_two, preferred_element_type=jnp.float32)
        exponent = jnp.exp(logits)
        probability = exponent / jnp.sum(exponent, axis=1, keepdims=True)
        onehot_label = (label_ids[:, None] == jnp.arange(C, dtype=jnp.int32)[None, :]).astype(jnp.float32)
        d_logits = (probability - onehot_label).astype(jnp.bfloat16)
        grad_two = jnp.dot(hidden.T, d_logits, preferred_element_type=jnp.float32)
        d_hidden = jnp.dot(d_logits, w_two.T, preferred_element_type=jnp.float32).astype(jnp.bfloat16)
        scaled = weight_in.astype(jnp.float32)[:, :, None] * d_hidden.astype(jnp.float32)[:, None, :]
        positive = (pre_act > 0).astype(jnp.float32)
        d_pre = (scaled.reshape(TGT_DEV * K, H) * positive).astype(jnp.bfloat16)
        grad_one = jnp.dot(row_feats.T, d_pre, preferred_element_type=jnp.float32)
        return (totals[0] + grad_one, totals[1] + grad_two), None

    start = (jnp.zeros((F, H), jnp.float32), jnp.zeros((H, C), jnp.float32))
    totals, unused = lax.scan(one_block, start, (pages_in, weights_in, labels_in))
    return (totals[0], totals[1])
```

```python
import functools
import jax
import jax.numpy as jnp
from jax import lax
from jax.experimental import pallas as pl
from jax.experimental.pallas import tpu as pltpu
from jax.sharding import PartitionSpec as P

GROUP = 8
LOW = 256
NT = (((1,), (1,)), ((), ()))
VMEM_LIMIT = 56 * 1024 * 1024


def dot(a, b):
    return jnp.dot(a, b, preferred_element_type=jnp.float32)


def dot_nt(a, b):
    return lax.dot_general(a, b, NT, preferred_element_type=jnp.float32)


def build_spread(page_ref, weight_ref, first_row, rows_dev, spread_ref, chunk):
    span = page_ref.shape[1]
    width_k = span // GROUP
    high = rows_dev // LOW
    local = page_ref[...] - first_row
    here = (local >= 0) & (local < rows_dev)
    lane_target = lax.broadcasted_iota(jnp.int32, local.shape, 1) // width_k
    key = jnp.where(here, (local // LOW) * GROUP + lane_target, -1).astype(jnp.float32)
    low = jnp.where(here, local % LOW, -1).astype(jnp.float32)
    key = key.astype(jnp.bfloat16)
    low = low.astype(jnp.bfloat16)
    weight = weight_ref[...]
    zero = jnp.zeros((), jnp.bfloat16)
    one = jnp.ones((), jnp.bfloat16)
    key_rows = lax.broadcasted_iota(jnp.int32, (high * GROUP, span), 0).astype(jnp.float32).astype(jnp.bfloat16)
    low_rows = lax.broadcasted_iota(jnp.int32, (LOW, span), 0).astype(jnp.float32).astype(jnp.bfloat16)
    for pair in range(chunk // (2 * GROUP)):
        parts = []
        for g in (2 * pair, 2 * pair + 1):
            left = jnp.where(key_rows == key[g : g + 1, :], weight[g : g + 1, :], zero)
            right = jnp.where(low_rows == low[g : g + 1, :], one, zero)
            parts.append(dot_nt(left, right))
        for h in range(high):
            rows = [p[h * GROUP : (h + 1) * GROUP, :] for p in parts]
            spread_ref[2 * GROUP * pair : 2 * GROUP * (pair + 1), h * LOW : (h + 1) * LOW] = (
                jnp.concatenate(rows, axis=0).astype(jnp.bfloat16)
            )


def forward_kernel(own_axes, page_ref, weight_ref, feat_ref, w_one_t_ref, w_two_t_ref,
                   active_ref, spread_ref, hidden_ref, logit_ref):
    rows_dev = feat_ref.shape[0]
    chunk = spread_ref.shape[0]
    first_row = lax.axis_index(own_axes) * rows_dev

    @pl.when(pl.program_id(0) == 0)
    def _():
        def tile(i, _):
            at = pl.ds(pl.multiple_of(i * 512, 512), 512)
            pre = dot_nt(w_one_t_ref[...], feat_ref[at, :])
            active_ref[:, at] = jnp.maximum(pre, 0.0).astype(jnp.bfloat16)
            return 0
        lax.fori_loop(0, rows_dev // 512, tile, 0)

    build_spread(page_ref, weight_ref, first_row, rows_dev, spread_ref, chunk)
    hidden = dot_nt(active_ref[...], spread_ref[...]).astype(jnp.bfloat16)
    hidden_ref[...] = hidden
    logit_ref[...] = dot(w_two_t_ref[...], hidden)


def forward(own_axes, pages, weights, features, w_one_t, w_two_t):
    rows_dev, width_f = features.shape
    units = w_one_t.shape[0]
    classes = w_two_t.shape[0]
    groups, span = pages.shape
    targets = groups * GROUP
    chunk = min(256, targets)
    steps = targets // chunk
    whole = lambda shape: pl.BlockSpec(shape, lambda i: (0, 0))
    return pl.pallas_call(
        functools.partial(forward_kernel, own_axes),
        grid=(steps,),
        in_specs=[
            pl.BlockSpec((chunk // GROUP, span), lambda i: (i, 0)),
            pl.BlockSpec((chunk // GROUP, span), lambda i: (i, 0)),
            whole((rows_dev, width_f)),
            whole((units, width_f)),
            whole((classes, units)),
        ],
        out_specs=[
            whole((units, rows_dev)),
            pl.BlockSpec((chunk, rows_dev), lambda i: (i, 0)),
            pl.BlockSpec((units, chunk), lambda i: (0, i)),
            pl.BlockSpec((classes, chunk), lambda i: (0, i)),
        ],
        out_shape=[
            jax.ShapeDtypeStruct((units, rows_dev), jnp.bfloat16),
            jax.ShapeDtypeStruct((targets, rows_dev), jnp.bfloat16),
            jax.ShapeDtypeStruct((units, targets), jnp.bfloat16),
            jax.ShapeDtypeStruct((classes, targets), jnp.float32),
        ],
        compiler_params=pltpu.CompilerParams(vmem_limit_bytes=VMEM_LIMIT),
    )(pages, weights, features, w_one_t, w_two_t)


def backward_kernel(dlog_ref, hidden_ref, w_two_ref, spread_ref, active_ref, feat_ref,
                    grad_one_ref, grad_two_ref, d_hidden, total):
    step = pl.program_id(0)

    @pl.when(step == 0)
    def _():
        d_hidden[...] = dot(w_two_ref[...], dlog_ref[...]).astype(jnp.bfloat16)
        grad_two_ref[...] = dot_nt(hidden_ref[...], dlog_ref[...])
        total[...] = jnp.zeros_like(total)

    spread_grad = dot(d_hidden[...], spread_ref[...])
    d_pre = jnp.where(active_ref[...] > 0, spread_grad, 0.0).astype(jnp.bfloat16)
    total[...] += dot(d_pre, feat_ref[...])

    @pl.when(step == pl.num_programs(0) - 1)
    def _():
        grad_one_ref[...] = total[...].T


def backward(dlog_t, hidden_t, w_two, spread, active_t, features):
    rows_dev, width_f = features.shape
    units, classes = w_two.shape
    targets = spread.shape[0]
    block = 512
    whole = lambda shape: pl.BlockSpec(shape, lambda i: (0, 0))
    return pl.pallas_call(
        backward_kernel,
        grid=(rows_dev // block,),
        in_specs=[
            whole((classes, targets)),
            whole((units, targets)),
            whole((units, classes)),
            pl.BlockSpec((targets, block), lambda i: (0, i)),
            pl.BlockSpec((units, block), lambda i: (0, i)),
            pl.BlockSpec((block, width_f), lambda i: (i, 0)),
        ],
        out_specs=[whole((width_f, units)), whole((units, classes))],
        out_shape=[
            jax.ShapeDtypeStruct((width_f, units), jnp.float32),
            jax.ShapeDtypeStruct((units, classes), jnp.float32),
        ],
        scratch_shapes=[
            pltpu.VMEM((units, targets), jnp.bfloat16),
            pltpu.VMEM((units, width_f), jnp.float32),
        ],
        compiler_params=pltpu.CompilerParams(vmem_limit_bytes=VMEM_LIMIT),
    )(dlog_t, hidden_t, w_two, spread, active_t, features)


def body(features, nbr_page, nbr_weight, labels, w_one, w_two):
    own_axes = ("own", "col")
    targets_dev, width_k = nbr_page.shape
    span = GROUP * width_k
    pages = lax.all_gather(nbr_page.reshape(-1, span), own_axes, axis=0, tiled=True)
    weights = lax.all_gather(nbr_weight.reshape(-1, span), own_axes, axis=0, tiled=True)
    all_labels = lax.all_gather(labels, own_axes, axis=0, tiled=True)
    active_t, spread, hidden_t, part_t = forward(own_axes, pages, weights, features, w_one.T, w_two.T)
    logits = lax.psum(part_t, ("own", "col", "mlp"))
    exponent = jnp.exp(logits)
    probability = exponent / jnp.sum(exponent, axis=0, keepdims=True)
    classes = w_two.shape[1]
    onehot = (jnp.arange(classes, dtype=jnp.int32)[:, None] == all_labels[None, :]).astype(jnp.float32)
    dlog_t = (probability - onehot).astype(jnp.bfloat16)
    grad_one, grad_two = backward(dlog_t, hidden_t, w_two, spread, active_t, features)
    return lax.psum((grad_one, grad_two), own_axes)


def solution(mesh):
    placed = (
        P(("own", "col"), None),
        P(("own", "col"), None),
        P(("own", "col"), None),
        P(("own", "col")),
        P(None, "mlp"),
        P("mlp", None),
    )
    return jax.shard_map(
        body,
        mesh=mesh,
        in_specs=placed,
        out_specs=(P(None, "mlp"), P("mlp", None)),
        check_vma=False,
    )
```

```python
import functools
import jax
import jax.numpy as jnp
from jax import lax
from jax.experimental import pallas as pl
from jax.experimental.pallas import tpu as pltpu
from jax.sharding import PartitionSpec as P

GROUP = 8
LOW = 256
LANES = 128
NT = (((1,), (1,)), ((), ()))
VMEM_LIMIT = 56 * 1024 * 1024


def dot(a, b):
    return jnp.dot(a, b, preferred_element_type=jnp.float32)


def dot_nt(a, b):
    return lax.dot_general(a, b, NT, preferred_element_type=jnp.float32)


MESH = pl.DeviceIdType.MESH


def split_axis(axis, parts):
    size = lax.axis_size(axis)
    steps, stride = [], 1
    for members in parts:
        members = size // stride if members is None else min(members, size // stride)
        if members > 1:
            steps.append((axis, members, stride))
        stride *= members
    return steps


def place(step):
    axis, members, stride = step
    return lax.rem(lax.div(lax.axis_index(axis), stride), members)


def partner(step, shift):
    axis, members, stride = step
    mine = place(step)
    other = lax.rem(mine + shift, members)
    return other, {axis: lax.axis_index(axis) + (other - mine) * stride}


def greet(steps):
    barrier = pltpu.get_barrier_semaphore()
    count = 0
    for step in steps:
        for shift in range(1, step[1]):
            pl.semaphore_signal(barrier, inc=1, device_id=partner(step, shift)[1], device_id_type=MESH)
            count += 1
    pl.semaphore_wait(barrier, count)


def start_scatter(step, piece, held, recv, sems, started):
    copies = []
    for shift in range(1, step[1]):
        other, device = partner(step, shift)
        copy = pltpu.make_async_remote_copy(
            src_ref=held.at[piece, :, other], dst_ref=recv.at[piece, shift - 1],
            send_sem=sems[0].at[piece, shift - 1], recv_sem=sems[1].at[piece, shift - 1],
            device_id=device, device_id_type=MESH)
        copy.start()
        copies.append(copy)
    started.extend(copies)
    return copies


def start_gather(steps, k, piece, full, sems, started):
    where = (piece,) + (slice(None),) * (len(steps) - 1 - k) + tuple(place(s) for s in reversed(steps[: k + 1]))
    copies = []
    for shift in range(1, steps[k][1]):
        copy = pltpu.make_async_remote_copy(
            src_ref=full.at[where], dst_ref=full.at[where],
            send_sem=sems[0].at[piece, shift - 1], recv_sem=sems[1].at[piece, shift - 1],
            device_id=partner(steps[k], shift)[1], device_id_type=MESH)
        copy.start()
        copies.append(copy)
    started.extend(copies)
    return copies


def settle(copies):
    for copy in copies:
        copy.wait_recv()


def sum_kernel(steps, pieces, finish, n_extra, *refs):
    first = refs[0]
    extra = refs[1 : 1 + n_extra]
    full = refs[1 + n_extra]
    scratch = refs[2 + n_extra :]
    count = len(steps)
    recv, held = scratch[:count], (first,) + scratch[count : 2 * count - 1]
    sems = scratch[2 * count - 1 :]
    scatter_sems = [(sems[2 * k], sems[2 * k + 1]) for k in range(count)]
    gather_sems = [(sems[2 * (count + k)], sems[2 * (count + k) + 1]) for k in range(count)]
    greet(steps)
    started = []
    flying = [start_scatter(steps[0], p, held[0], recv[0], scatter_sems[0], started) for p in range(pieces)]
    last = []
    for k in range(count):
        following = []
        for p in range(pieces):
            settle(flying[p])
            total = held[k][p, :, place(steps[k])].astype(jnp.float32)
            for j in range(steps[k][1] - 1):
                total = total + recv[k][p, j].astype(jnp.float32)
            if k + 1 < count:
                held[k + 1][p] = total.astype(jnp.bfloat16).reshape(held[k + 1].shape[1:])
                following.append(start_scatter(steps[k + 1], p, held[k + 1], recv[k + 1], scatter_sems[k + 1], started))
            else:
                last.append(total.reshape(total.shape[1:]))
                if finish is None:
                    full[(p,) + tuple(place(s) for s in reversed(steps))] = last[p].astype(jnp.bfloat16)
                    following.append(start_gather(steps, k, p, full, gather_sems[k], started))
        flying = following
    if finish is not None:
        results = finish(last, *extra)
        for p in range(pieces):
            full[(p,) + tuple(place(s) for s in reversed(steps))] = results[p].astype(jnp.bfloat16)
            flying.append(start_gather(steps, count - 1, p, full, gather_sems[count - 1], started))
    for k in range(count - 2, -1, -1):
        following = []
        for p in range(pieces):
            settle(flying[p])
            following.append(start_gather(steps, k, p, full, gather_sems[k], started))
        flying = following
    for p in range(pieces):
        settle(flying[p])
    for copy in started:
        copy.wait_send()


def sum_blocks(array, steps, collective_id, finish=None, extra=()):
    pieces, rows, lanes = array.shape
    sizes = [s[1] for s in steps]
    block = rows
    for size in sizes:
        block //= size
    recv, held, outer = [], [], rows // block
    for k, size in enumerate(sizes):
        outer //= size
        if k == 0:
            first = array.reshape(pieces, outer, size, block, lanes)
        else:
            held.append(pltpu.VMEM((pieces, outer, size, block, lanes), jnp.bfloat16))
        recv.append(pltpu.VMEM((pieces, size - 1, outer, block, lanes), jnp.bfloat16))
    sems = [pltpu.SemaphoreType.DMA((pieces, size - 1)) for size in sizes for _ in range(2)] * 2
    vmem = pl.BlockSpec(memory_space=pltpu.VMEM)
    full = pl.pallas_call(
        functools.partial(sum_kernel, steps, pieces, finish, len(extra)),
        in_specs=[vmem] * (1 + len(extra)),
        out_specs=vmem,
        out_shape=jax.ShapeDtypeStruct((pieces, *reversed(sizes), block, lanes), jnp.bfloat16),
        scratch_shapes=recv + held + sems,
        compiler_params=pltpu.CompilerParams(
            collective_id=collective_id, has_side_effects=True, vmem_limit_bytes=VMEM_LIMIT),
    )(first, *extra)
    return full.reshape(pieces, rows, lanes)


def gather_kernel(steps, *refs):
    count = len(refs) // 3
    ins, outs, sems = refs[:count], refs[count : 2 * count], refs[2 * count :]
    where = (0,) + tuple(place(s) for s in reversed(steps))
    greet(steps)
    started = []
    for a in range(count):
        outs[a][where] = ins[a][...]
    for k in range(len(steps) - 1, -1, -1):
        flying = []
        for a in range(count):
            pair = (sems[a].at[k, 0], sems[a].at[k, 1])
            flying.extend(start_gather(steps, k, 0, outs[a], pair, started))
        settle(flying)
    for copy in started:
        copy.wait_send()


def gather_blocks(arrays, steps, collective_id):
    sizes = [s[1] for s in steps]
    vmem = pl.BlockSpec(memory_space=pltpu.VMEM)
    outs = pl.pallas_call(
        functools.partial(gather_kernel, steps),
        in_specs=[vmem] * len(arrays),
        out_specs=[vmem] * len(arrays),
        out_shape=[jax.ShapeDtypeStruct((1, *reversed(sizes), *a.shape), a.dtype) for a in arrays],
        scratch_shapes=[pltpu.SemaphoreType.DMA((len(steps), 2, 1, max(sizes) - 1))] * len(arrays),
        compiler_params=pltpu.CompilerParams(
            collective_id=collective_id, has_side_effects=True, vmem_limit_bytes=VMEM_LIMIT),
    )(*arrays)
    return [o.reshape(-1, o.shape[-1]) for o in outs]


def softmax_gradient(logits, label_ref):
    lanes = logits[0].shape[1]
    rows = logits[0].shape[0]
    start = pl.multiple_of(lax.axis_index("mlp") * rows, rows)
    label = label_ref[pl.ds(start, rows), :]
    exponent = [jnp.exp(x) for x in logits]
    total = sum(jnp.sum(e, axis=1, keepdims=True) for e in exponent)
    results = []
    for p, e in enumerate(exponent):
        category = lax.broadcasted_iota(jnp.int32, e.shape, 1) + p * lanes
        results.append(e / total - jnp.where(category == label, 1.0, 0.0))
    return results


def build_spread(page_ref, weight_ref, first_row, rows_dev, spread_ref, chunk):
    span = page_ref.shape[1]
    width_k = span // GROUP
    high = rows_dev // LOW
    local = page_ref[...] - first_row
    here = (local >= 0) & (local < rows_dev)
    lane_target = lax.broadcasted_iota(jnp.int32, local.shape, 1) // width_k
    key = jnp.where(here, (local // LOW) * GROUP + lane_target, -1).astype(jnp.float32)
    low = jnp.where(here, local % LOW, -1).astype(jnp.float32)
    key = key.astype(jnp.bfloat16)
    low = low.astype(jnp.bfloat16)
    weight = weight_ref[...]
    zero = jnp.zeros((), jnp.bfloat16)
    one = jnp.ones((), jnp.bfloat16)
    key_rows = lax.broadcasted_iota(jnp.int32, (high * GROUP, span), 0).astype(jnp.float32).astype(jnp.bfloat16)
    low_rows = lax.broadcasted_iota(jnp.int32, (LOW, span), 0).astype(jnp.float32).astype(jnp.bfloat16)
    for pair in range(chunk // (2 * GROUP)):
        parts = []
        for g in (2 * pair, 2 * pair + 1):
            left = jnp.where(key_rows == key[g : g + 1, :], weight[g : g + 1, :], zero)
            right = jnp.where(low_rows == low[g : g + 1, :], one, zero)
            parts.append(dot_nt(left, right))
        for h in range(high):
            rows = [p[h * GROUP : (h + 1) * GROUP, :] for p in parts]
            spread_ref[2 * GROUP * pair : 2 * GROUP * (pair + 1), h * LOW : (h + 1) * LOW] = (
                jnp.concatenate(rows, axis=0).astype(jnp.bfloat16)
            )


def forward_kernel(own_axes, page_ref, weight_ref, feat_ref, w_one_t_ref, w_two_t_ref,
                   active_ref, spread_ref, hidden_ref, logit_ref):
    rows_dev = feat_ref.shape[0]
    chunk = spread_ref.shape[0]
    first_row = lax.axis_index(own_axes) * rows_dev

    @pl.when(pl.program_id(0) == 0)
    def _():
        def tile(i, _):
            at = pl.ds(pl.multiple_of(i * 512, 512), 512)
            pre = dot_nt(w_one_t_ref[...], feat_ref[at, :])
            active_ref[:, at] = jnp.maximum(pre, 0.0).astype(jnp.bfloat16)
            return 0
        lax.fori_loop(0, rows_dev // 512, tile, 0)

    build_spread(page_ref, weight_ref, first_row, rows_dev, spread_ref, chunk)
    hidden = dot_nt(active_ref[...], spread_ref[...]).astype(jnp.bfloat16)
    hidden_ref[...] = hidden
    logits = dot(w_two_t_ref[...], hidden).T.astype(jnp.bfloat16)
    lanes = logit_ref.shape[2]
    for p in range(logit_ref.shape[0]):
        logit_ref[p] = logits[:, p * lanes : (p + 1) * lanes]


def forward(own_axes, pages, weights, features, w_one_t, w_two_t):
    rows_dev, width_f = features.shape
    units = w_one_t.shape[0]
    classes = w_two_t.shape[0]
    groups, span = pages.shape
    targets = groups * GROUP
    chunk = min(256, targets)
    steps = targets // chunk
    whole = lambda shape: pl.BlockSpec(shape, lambda i: (0, 0))
    return pl.pallas_call(
        functools.partial(forward_kernel, own_axes),
        grid=(steps,),
        in_specs=[
            pl.BlockSpec((chunk // GROUP, span), lambda i: (i, 0)),
            pl.BlockSpec((chunk // GROUP, span), lambda i: (i, 0)),
            whole((rows_dev, width_f)),
            whole((units, width_f)),
            whole((classes, units)),
        ],
        out_specs=[
            whole((units, rows_dev)),
            pl.BlockSpec((chunk, rows_dev), lambda i: (i, 0)),
            pl.BlockSpec((units, chunk), lambda i: (0, i)),
            pl.BlockSpec((classes // LANES, chunk, LANES), lambda i: (0, i, 0)),
        ],
        out_shape=[
            jax.ShapeDtypeStruct((units, rows_dev), jnp.bfloat16),
            jax.ShapeDtypeStruct((targets, rows_dev), jnp.bfloat16),
            jax.ShapeDtypeStruct((units, targets), jnp.bfloat16),
            jax.ShapeDtypeStruct((classes // LANES, targets, LANES), jnp.bfloat16),
        ],
        compiler_params=pltpu.CompilerParams(vmem_limit_bytes=VMEM_LIMIT),
    )(pages, weights, features, w_one_t, w_two_t)


def backward_kernel(dlog_ref, hidden_ref, w_two_ref, spread_ref, active_ref, feat_ref,
                    grad_ref, d_hidden, total):
    step = pl.program_id(0)
    units = total.shape[0]
    width_f = total.shape[1]
    ones = units // LANES

    @pl.when(step == 0)
    def _():
        d_logits = jnp.concatenate([dlog_ref[p] for p in range(dlog_ref.shape[0])], axis=1)
        d_hidden[...] = dot_nt(w_two_ref[...], d_logits).astype(jnp.bfloat16)
        grad_two = dot(hidden_ref[...], d_logits).astype(jnp.bfloat16)
        for p in range(grad_two.shape[1] // LANES):
            grad_ref[ones + p] = grad_two[:, p * LANES : (p + 1) * LANES]
        total[...] = jnp.zeros_like(total)

    spread_grad = dot(d_hidden[...], spread_ref[...])
    d_pre = jnp.where(active_ref[...] > 0, spread_grad, 0.0).astype(jnp.bfloat16)
    total[...] += dot(d_pre, feat_ref[...])

    @pl.when(step == pl.num_programs(0) - 1)
    def _():
        for p in range(ones):
            grad_ref[p] = total[p * LANES : (p + 1) * LANES, :].T.astype(jnp.bfloat16)


def backward(dlog, hidden_t, w_two, spread, active_t, features):
    rows_dev, width_f = features.shape
    units, classes = w_two.shape
    assert units == width_f
    targets = spread.shape[0]
    block = 512
    whole = lambda shape: pl.BlockSpec(shape, lambda i: (0,) * len(shape))
    out = ((units + classes) // LANES, width_f, LANES)
    return pl.pallas_call(
        backward_kernel,
        grid=(rows_dev // block,),
        in_specs=[
            whole(dlog.shape),
            whole((units, targets)),
            whole((units, classes)),
            pl.BlockSpec((targets, block), lambda i: (0, i)),
            pl.BlockSpec((units, block), lambda i: (0, i)),
            pl.BlockSpec((block, width_f), lambda i: (i, 0)),
        ],
        out_specs=whole(out),
        out_shape=jax.ShapeDtypeStruct(out, jnp.bfloat16),
        scratch_shapes=[
            pltpu.VMEM((units, targets), jnp.bfloat16),
            pltpu.VMEM((units, width_f), jnp.float32),
        ],
        compiler_params=pltpu.CompilerParams(vmem_limit_bytes=VMEM_LIMIT),
    )(dlog, hidden_t, w_two, spread, active_t, features)


def body(features, nbr_page, nbr_weight, labels, w_one, w_two):
    own_axes = ("own", "col")
    units, classes = w_two.shape
    targets_dev, width_k = nbr_page.shape
    span = GROUP * width_k
    owner_steps = split_axis("col", (2, None)) + split_axis("own", (None,))
    all_steps = split_axis("mlp", (2, None)) + owner_steps
    pages, weights = gather_blocks(
        (nbr_page.reshape(-1, span), nbr_weight.reshape(-1, span)), owner_steps, 0)
    active_t, spread, hidden_t, part = forward(own_axes, pages, weights, features, w_one.T, w_two.T)
    dlog = sum_blocks(part, all_steps, 1, softmax_gradient, (labels[:, None],))
    grads = backward(dlog, hidden_t, w_two, spread, active_t, features)
    grads = sum_blocks(grads, owner_steps, 2).astype(jnp.float32)
    ones = units // LANES
    grad_one = jnp.concatenate([grads[p] for p in range(ones)], axis=1)
    grad_two = jnp.concatenate([grads[p] for p in range(ones, grads.shape[0])], axis=1)
    return grad_one, grad_two


def solution(mesh):
    placed = (
        P(("own", "col"), None),
        P(("own", "col"), None),
        P(("own", "col"), None),
        P(("own", "col")),
        P(None, "mlp"),
        P("mlp", None),
    )
    return jax.shard_map(
        body,
        mesh=mesh,
        in_specs=placed,
        out_specs=(P(None, "mlp"), P("mlp", None)),
        check_vma=False,
    )
```

```python
import functools
import jax
import jax.numpy as jnp
from jax import lax
from jax.experimental import pallas as pl
from jax.experimental.pallas import tpu as pltpu
from jax.sharding import PartitionSpec as P

GROUP = 8
LOW = 256
LANES = 128
SPREAD_LIMIT = 8 * 1024 * 1024
NT = (((1,), (1,)), ((), ()))
VMEM_LIMIT = 56 * 1024 * 1024


def dot(a, b):
    return jnp.dot(a, b, preferred_element_type=jnp.float32)


def dot_nt(a, b):
    return lax.dot_general(a, b, NT, preferred_element_type=jnp.float32)


MESH = pl.DeviceIdType.MESH


def split_axis(axis, parts):
    size = lax.axis_size(axis)
    steps, stride = [], 1
    for members in parts:
        members = size // stride if members is None else min(members, size // stride)
        if members > 1:
            steps.append((axis, members, stride))
        stride *= members
    return steps


def place(step):
    axis, members, stride = step
    return lax.rem(lax.div(lax.axis_index(axis), stride), members)


def partner(step, shift):
    axis, members, stride = step
    mine = place(step)
    other = lax.rem(mine + shift, members)
    return other, {axis: lax.axis_index(axis) + (other - mine) * stride}


def greet(steps):
    barrier = pltpu.get_barrier_semaphore()
    count = 0
    for step in steps:
        for shift in range(1, step[1]):
            pl.semaphore_signal(barrier, inc=1, device_id=partner(step, shift)[1], device_id_type=MESH)
            count += 1
    pl.semaphore_wait(barrier, count)


def start_scatter(step, piece, held, recv, sems, started):
    copies = []
    for shift in range(1, step[1]):
        other, device = partner(step, shift)
        copy = pltpu.make_async_remote_copy(
            src_ref=held.at[piece, :, other], dst_ref=recv.at[piece, shift - 1],
            send_sem=sems[0].at[piece, shift - 1], recv_sem=sems[1].at[piece, shift - 1],
            device_id=device, device_id_type=MESH)
        copy.start()
        copies.append(copy)
    started.extend(copies)
    return copies


def start_gather(steps, k, piece, full, sems, started):
    where = (piece,) + (slice(None),) * (len(steps) - 1 - k) + tuple(place(s) for s in reversed(steps[: k + 1]))
    copies = []
    for shift in range(1, steps[k][1]):
        copy = pltpu.make_async_remote_copy(
            src_ref=full.at[where], dst_ref=full.at[where],
            send_sem=sems[0].at[piece, shift - 1], recv_sem=sems[1].at[piece, shift - 1],
            device_id=partner(steps[k], shift)[1], device_id_type=MESH)
        copy.start()
        copies.append(copy)
    started.extend(copies)
    return copies


def settle(copies):
    for copy in copies:
        copy.wait_recv()


def sum_kernel(steps, pieces, finish, n_extra, *refs):
    first = refs[0]
    extra = refs[1 : 1 + n_extra]
    full = refs[1 + n_extra]
    scratch = refs[2 + n_extra :]
    count = len(steps)
    recv, held = scratch[:count], (first,) + scratch[count : 2 * count - 1]
    sems = scratch[2 * count - 1 :]
    scatter_sems = [(sems[2 * k], sems[2 * k + 1]) for k in range(count)]
    gather_sems = [(sems[2 * (count + k)], sems[2 * (count + k) + 1]) for k in range(count)]
    greet(steps)
    started = []
    flying = [start_scatter(steps[0], p, held[0], recv[0], scatter_sems[0], started) for p in range(pieces)]
    last = []
    for k in range(count):
        following = []
        for p in range(pieces):
            settle(flying[p])
            total = held[k][p, :, place(steps[k])].astype(jnp.float32)
            for j in range(steps[k][1] - 1):
                total = total + recv[k][p, j].astype(jnp.float32)
            if k + 1 < count:
                held[k + 1][p] = total.astype(jnp.bfloat16).reshape(held[k + 1].shape[1:])
                following.append(start_scatter(steps[k + 1], p, held[k + 1], recv[k + 1], scatter_sems[k + 1], started))
            else:
                last.append(total.reshape(total.shape[1:]))
                if finish is None:
                    full[(p,) + tuple(place(s) for s in reversed(steps))] = last[p].astype(jnp.bfloat16)
                    following.append(start_gather(steps, k, p, full, gather_sems[k], started))
        flying = following
    if finish is not None:
        results = finish(last, *extra)
        for p in range(pieces):
            full[(p,) + tuple(place(s) for s in reversed(steps))] = results[p].astype(jnp.bfloat16)
            flying.append(start_gather(steps, count - 1, p, full, gather_sems[count - 1], started))
    for k in range(count - 2, -1, -1):
        following = []
        for p in range(pieces):
            settle(flying[p])
            following.append(start_gather(steps, k, p, full, gather_sems[k], started))
        flying = following
    for p in range(pieces):
        settle(flying[p])
    for copy in started:
        copy.wait_send()


def sum_blocks(array, steps, collective_id, finish=None, extra=()):
    pieces, rows, lanes = array.shape
    sizes = [s[1] for s in steps]
    block = rows
    for size in sizes:
        block //= size
    recv, held, outer = [], [], rows // block
    for k, size in enumerate(sizes):
        outer //= size
        if k == 0:
            first = array.reshape(pieces, outer, size, block, lanes)
        else:
            held.append(pltpu.VMEM((pieces, outer, size, block, lanes), jnp.bfloat16))
        recv.append(pltpu.VMEM((pieces, size - 1, outer, block, lanes), jnp.bfloat16))
    sems = [pltpu.SemaphoreType.DMA((pieces, size - 1)) for size in sizes for _ in range(2)] * 2
    vmem = pl.BlockSpec(memory_space=pltpu.VMEM)
    full = pl.pallas_call(
        functools.partial(sum_kernel, steps, pieces, finish, len(extra)),
        in_specs=[vmem] * (1 + len(extra)),
        out_specs=vmem,
        out_shape=jax.ShapeDtypeStruct((pieces, *reversed(sizes), block, lanes), jnp.bfloat16),
        scratch_shapes=recv + held + sems,
        compiler_params=pltpu.CompilerParams(
            collective_id=collective_id, has_side_effects=True, vmem_limit_bytes=VMEM_LIMIT),
    )(first, *extra)
    return full.reshape(pieces, rows, lanes)


def gather_kernel(steps, *refs):
    count = len(refs) // 3
    ins, outs, sems = refs[:count], refs[count : 2 * count], refs[2 * count :]
    where = (0,) + tuple(place(s) for s in reversed(steps))
    greet(steps)
    started = []
    for a in range(count):
        outs[a][where] = ins[a][...]
    for k in range(len(steps) - 1, -1, -1):
        flying = []
        for a in range(count):
            pair = (sems[a].at[k, 0], sems[a].at[k, 1])
            flying.extend(start_gather(steps, k, 0, outs[a], pair, started))
        settle(flying)
    for copy in started:
        copy.wait_send()


def gather_blocks(arrays, steps, collective_id):
    sizes = [s[1] for s in steps]
    vmem = pl.BlockSpec(memory_space=pltpu.VMEM)
    outs = pl.pallas_call(
        functools.partial(gather_kernel, steps),
        in_specs=[vmem] * len(arrays),
        out_specs=[vmem] * len(arrays),
        out_shape=[jax.ShapeDtypeStruct((1, *reversed(sizes), *a.shape), a.dtype) for a in arrays],
        scratch_shapes=[pltpu.SemaphoreType.DMA((len(steps), 2, 1, max(sizes) - 1))] * len(arrays),
        compiler_params=pltpu.CompilerParams(
            collective_id=collective_id, has_side_effects=True, vmem_limit_bytes=VMEM_LIMIT),
    )(*arrays)
    return [o.reshape(-1, o.shape[-1]) for o in outs]


def softmax_gradient(logits, label_ref):
    lanes = logits[0].shape[1]
    rows = logits[0].shape[0]
    start = pl.multiple_of(lax.axis_index("mlp") * rows, rows)
    label = label_ref[pl.ds(start, rows), :]
    exponent = [jnp.exp(x) for x in logits]
    total = sum(jnp.sum(e, axis=1, keepdims=True) for e in exponent)
    results = []
    for p, e in enumerate(exponent):
        category = lax.broadcasted_iota(jnp.int32, e.shape, 1) + p * lanes
        results.append(e / total - jnp.where(category == label, 1.0, 0.0))
    return results


def build_spread(page_ref, weight_ref, first_row, rows_dev, spread_ref, chunk):
    span = page_ref.shape[1]
    width_k = span // GROUP
    high = rows_dev // LOW
    local = page_ref[...] - first_row
    here = (local >= 0) & (local < rows_dev)
    lane_target = lax.broadcasted_iota(jnp.int32, local.shape, 1) // width_k
    key = jnp.where(here, (local // LOW) * GROUP + lane_target, -1).astype(jnp.float32)
    low = jnp.where(here, local % LOW, -1).astype(jnp.float32)
    key = key.astype(jnp.bfloat16)
    low = low.astype(jnp.bfloat16)
    weight = weight_ref[...]
    zero = jnp.zeros((), jnp.bfloat16)
    one = jnp.ones((), jnp.bfloat16)
    key_rows = lax.broadcasted_iota(jnp.int32, (high * GROUP, span), 0).astype(jnp.float32).astype(jnp.bfloat16)
    low_rows = lax.broadcasted_iota(jnp.int32, (LOW, span), 0).astype(jnp.float32).astype(jnp.bfloat16)
    for pair in range(chunk // (2 * GROUP)):
        parts = []
        for g in (2 * pair, 2 * pair + 1):
            left = jnp.where(key_rows == key[g : g + 1, :], weight[g : g + 1, :], zero)
            right = jnp.where(low_rows == low[g : g + 1, :], one, zero)
            parts.append(dot_nt(left, right))
        for h in range(high):
            rows = [p[h * GROUP : (h + 1) * GROUP, :] for p in parts]
            spread_ref[2 * GROUP * pair : 2 * GROUP * (pair + 1), h * LOW : (h + 1) * LOW] = (
                jnp.concatenate(rows, axis=0).astype(jnp.bfloat16)
            )


def forward_kernel(own_axes, page_ref, weight_ref, feat_ref, w_one_t_ref, w_two_t_ref,
                   active_ref, spread_ref, hidden_ref, logit_ref):
    rows_dev = feat_ref.shape[0]
    chunk = spread_ref.shape[0]
    first_row = lax.axis_index(own_axes) * rows_dev

    @pl.when(pl.program_id(0) == 0)
    def _():
        def tile(i, _):
            at = pl.ds(pl.multiple_of(i * 512, 512), 512)
            pre = dot_nt(w_one_t_ref[...], feat_ref[at, :])
            active_ref[:, at] = jnp.maximum(pre, 0.0).astype(jnp.bfloat16)
            return 0
        lax.fori_loop(0, rows_dev // 512, tile, 0)

    build_spread(page_ref, weight_ref, first_row, rows_dev, spread_ref, chunk)
    hidden = dot_nt(active_ref[...], spread_ref[...]).astype(jnp.bfloat16)
    hidden_ref[...] = hidden
    logits = dot(w_two_t_ref[...], hidden).T.astype(jnp.bfloat16)
    lanes = logit_ref.shape[2]
    for p in range(logit_ref.shape[0]):
        logit_ref[p] = logits[:, p * lanes : (p + 1) * lanes]


def forward(own_axes, pages, weights, features, w_one_t, w_two_t):
    rows_dev, width_f = features.shape
    units = w_one_t.shape[0]
    classes = w_two_t.shape[0]
    groups, span = pages.shape
    targets = groups * GROUP
    chunk = min(256, targets)
    steps = targets // chunk
    whole = lambda shape: pl.BlockSpec(shape, lambda i: (0, 0))
    return pl.pallas_call(
        functools.partial(forward_kernel, own_axes),
        grid=(steps,),
        in_specs=[
            pl.BlockSpec((chunk // GROUP, span), lambda i: (i, 0)),
            pl.BlockSpec((chunk // GROUP, span), lambda i: (i, 0)),
            whole((rows_dev, width_f)),
            whole((units, width_f)),
            whole((classes, units)),
        ],
        out_specs=[
            whole((units, rows_dev)),
            pl.BlockSpec((chunk, rows_dev), lambda i: (i, 0)),
            pl.BlockSpec((units, chunk), lambda i: (0, i)),
            pl.BlockSpec((classes // LANES, chunk, LANES), lambda i: (0, i, 0)),
        ],
        out_shape=[
            jax.ShapeDtypeStruct((units, rows_dev), jnp.bfloat16),
            jax.ShapeDtypeStruct((targets, rows_dev), jnp.bfloat16),
            jax.ShapeDtypeStruct((units, targets), jnp.bfloat16),
            jax.ShapeDtypeStruct((classes // LANES, targets, LANES), jnp.bfloat16),
        ],
        compiler_params=pltpu.CompilerParams(vmem_limit_bytes=VMEM_LIMIT),
    )(pages, weights, features, w_one_t, w_two_t)


def backward_kernel(dlog_ref, hidden_ref, w_two_ref, spread_ref, active_ref, feat_ref,
                    grad_ref, d_hidden, total):
    step = pl.program_id(0)
    units = total.shape[0]
    width_f = total.shape[1]
    ones = units // LANES

    @pl.when(step == 0)
    def _():
        d_logits = jnp.concatenate([dlog_ref[p] for p in range(dlog_ref.shape[0])], axis=1)
        d_hidden[...] = dot_nt(w_two_ref[...], d_logits).astype(jnp.bfloat16)
        grad_two = dot(hidden_ref[...], d_logits).astype(jnp.bfloat16)
        for p in range(grad_two.shape[1] // LANES):
            grad_ref[ones + p] = grad_two[:, p * LANES : (p + 1) * LANES]
        total[...] = jnp.zeros_like(total)

    spread_grad = dot(d_hidden[...], spread_ref[...])
    d_pre = jnp.where(active_ref[...] > 0, spread_grad, 0.0).astype(jnp.bfloat16)
    total[...] += dot(d_pre, feat_ref[...])

    @pl.when(step == pl.num_programs(0) - 1)
    def _():
        for p in range(ones):
            grad_ref[p] = total[p * LANES : (p + 1) * LANES, :].T.astype(jnp.bfloat16)


def backward(dlog, hidden_t, w_two, spread, active_t, features):
    rows_dev, width_f = features.shape
    units, classes = w_two.shape
    assert units == width_f
    targets = spread.shape[0]
    block = 512
    whole = lambda shape: pl.BlockSpec(shape, lambda i: (0,) * len(shape))
    out = ((units + classes) // LANES, width_f, LANES)
    return pl.pallas_call(
        backward_kernel,
        grid=(rows_dev // block,),
        in_specs=[
            whole(dlog.shape),
            whole((units, targets)),
            whole((units, classes)),
            pl.BlockSpec((targets, block), lambda i: (0, i)),
            pl.BlockSpec((units, block), lambda i: (0, i)),
            pl.BlockSpec((block, width_f), lambda i: (i, 0)),
        ],
        out_specs=whole(out),
        out_shape=jax.ShapeDtypeStruct(out, jnp.bfloat16),
        scratch_shapes=[
            pltpu.VMEM((units, targets), jnp.bfloat16),
            pltpu.VMEM((units, width_f), jnp.float32),
        ],
        compiler_params=pltpu.CompilerParams(vmem_limit_bytes=VMEM_LIMIT),
    )(dlog, hidden_t, w_two, spread, active_t, features)


def scatter_total(step, piece, held, recv):
    total = held[piece, :, place(step)].astype(jnp.float32)
    for j in range(step[1] - 1):
        total = total + recv[piece, j].astype(jnp.float32)
    return total


def advance(running):
    for task in list(running):
        if next(task, "done") == "done":
            running.remove(task)


def fused_kernel(plan, *refs):
    it = iter(refs)
    packed_ref, label_ref, feat_ref, w_one_ref, w_two_ref, one_ref, two_ref = (next(it) for _ in range(7))
    pages_all, key_s, low_s, weight_s, active, spread, hidden, d_hidden, total = (next(it) for _ in range(9))
    inner, own, owner_steps, grad_steps = plan
    all_steps = inner + own
    chunks = own[0][1]
    held = [next(it) for _ in inner]
    recv = [next(it) for _ in inner]
    own_held, own_recv, full = (next(it) for _ in range(3))
    grad_held = [next(it) for _ in grad_steps]
    grad_recv = [next(it) for _ in grad_steps]
    grad_full = next(it)
    pairs = lambda n: [(next(it), next(it)) for _ in range(n)]
    page_sems = pairs(len(owner_steps))
    inner_sems = pairs(len(inner))
    own_sems = pairs(1)[0]
    full_sems = pairs(len(all_steps))
    scatter_sems = pairs(len(grad_steps))
    gather_sems = pairs(len(grad_steps))

    rows_dev, width_f = feat_ref.shape
    units, classes = w_two_ref.shape
    targets = spread.shape[0]
    chunk = targets // chunks
    span = key_s.shape[1]
    width_k = span // GROUP
    high = rows_dev // LOW
    started = []

    greet(all_steps)
    pages_all[(0,) + tuple(place(s) for s in reversed(owner_steps))] = packed_ref[...]
    w_one_t = w_one_ref[...].T
    stages = len(owner_steps)
    tiles = rows_dev // 512
    for k in range(stages - 1, -1, -1):
        flying = start_gather(owner_steps, k, 0, pages_all, page_sems[k], started)
        done = stages - 1 - k
        for i in range(done * tiles // stages, (done + 1) * tiles // stages):
            pre = dot_nt(w_one_t, feat_ref[i * 512 : (i + 1) * 512, :])
            active[:, i * 512 : (i + 1) * 512] = jnp.maximum(pre, 0.0).astype(jnp.bfloat16)
        settle(flying)

    lists = pages_all[0]
    lead = (slice(None),) * stages
    page = lists[lead + (0,)].reshape(-1, span)
    weight_s[...] = lists[lead + (1,)].reshape(-1, span)
    local = page.astype(jnp.int32) - lax.axis_index(("own", "col")) * rows_dev
    here = (local >= 0) & (local < rows_dev)
    lane_target = lax.broadcasted_iota(jnp.int32, local.shape, 1) // width_k
    key_s[...] = jnp.where(here, (local // LOW) * GROUP + lane_target, -1).astype(jnp.float32)
    low_s[...] = jnp.where(here, local % LOW, -1).astype(jnp.float32)

    zero = jnp.zeros((), jnp.bfloat16)
    one = jnp.ones((), jnp.bfloat16)
    key_rows = lax.broadcasted_iota(jnp.int32, (high * GROUP, span), 0).astype(jnp.float32).astype(jnp.bfloat16)
    low_rows = lax.broadcasted_iota(jnp.int32, (LOW, span), 0).astype(jnp.float32).astype(jnp.bfloat16)

    def build(i, carry):
        at = pl.ds(pl.multiple_of(i * 8, 8), 8)
        key = key_s[at, :].astype(jnp.bfloat16)
        low = low_s[at, :].astype(jnp.bfloat16)
        weight = weight_s[at, :].astype(jnp.bfloat16)
        for pair in range(4):
            parts = []
            for g in (2 * pair, 2 * pair + 1):
                left = jnp.where(key_rows == key[g : g + 1, :], weight[g : g + 1, :], zero)
                right = jnp.where(low_rows == low[g : g + 1, :], one, zero)
                parts.append(dot_nt(left, right))
            rows = pl.ds(pl.multiple_of(i * 64 + pair * 16, 16), 16)
            for h in range(high):
                both = [p[h * GROUP : (h + 1) * GROUP, :] for p in parts]
                spread[rows, h * LOW : (h + 1) * LOW] = jnp.concatenate(both, axis=0).astype(jnp.bfloat16)
        return carry

    def sum_logits(c):
        for k, step in enumerate(inner):
            copies = start_scatter(step, c, held[k], recv[k], inner_sems[k], started)
            yield
            settle(copies)
            part = scatter_total(step, c, held[k], recv[k]).astype(jnp.bfloat16)
            if k + 1 < len(inner):
                held[k + 1][c] = part.reshape(held[k + 1].shape[1:])
            else:
                own_held[0, 0, c] = part[0]

    running = []
    w_two_t = w_two_ref[...].T
    blocks = chunk // 64
    for c in range(chunks):
        half = blocks // 2
        lax.fori_loop(c * blocks, c * blocks + half, build, 0)
        advance(running)
        lax.fori_loop(c * blocks + half, (c + 1) * blocks, build, 0)
        advance(running)
        block = dot_nt(active[...], spread[c * chunk : (c + 1) * chunk, :]).astype(jnp.bfloat16)
        hidden[:, c * chunk : (c + 1) * chunk] = block
        held[0][c] = dot(w_two_t, block).T.astype(jnp.bfloat16).reshape(held[0].shape[1:])
        advance(running)
        running.append(sum_logits(c))
        next(running[-1])
    while running:
        advance(running)
    settle(start_scatter(own[0], 0, own_held, own_recv, own_sems, started))
    logits = scatter_total(own[0], 0, own_held, own_recv)[0]
    d_logits = softmax_gradient([logits], label_ref)[0].astype(jnp.bfloat16)
    full[(0,) + tuple(place(s) for s in reversed(all_steps))] = d_logits
    for k in range(len(all_steps) - 1, -1, -1):
        settle(start_gather(all_steps, k, 0, full, full_sems[k], started))
    d_logits = full[0].reshape(targets, classes)

    def sum_grads(p, values):
        grad_held[0][p] = values.astype(jnp.bfloat16).reshape(grad_held[0].shape[1:])
        count = len(grad_steps)
        for k, step in enumerate(grad_steps):
            copies = start_scatter(step, p, grad_held[k], grad_recv[k], scatter_sems[k], started)
            yield
            settle(copies)
            part = scatter_total(step, p, grad_held[k], grad_recv[k]).astype(jnp.bfloat16)
            if k + 1 < count:
                grad_held[k + 1][p] = part.reshape(grad_held[k + 1].shape[1:])
        grad_full[(p,) + tuple(place(s) for s in reversed(grad_steps))] = part[0]
        for k in range(count - 1, -1, -1):
            copies = start_gather(grad_steps, k, p, grad_full, gather_sems[k], started)
            yield
            settle(copies)
        block = grad_full[p].reshape(width_f, LANES)
        if p < units // LANES:
            one_ref[:, p * LANES : (p + 1) * LANES] = block
        else:
            q = p - units // LANES
            two_ref[:, q * LANES : (q + 1) * LANES] = block

    def launch(p, values):
        running.append(sum_grads(p, values))
        next(running[-1])

    grad_two = dot(hidden[...], d_logits)
    for q in range(classes // LANES):
        launch(units // LANES + q, grad_two[:, q * LANES : (q + 1) * LANES])
    d_hidden[...] = dot_nt(w_two_ref[...], d_logits).astype(jnp.bfloat16)
    part_units = 256
    width_r = 1024
    for u in range(units // part_units):
        rows = slice(u * part_units, (u + 1) * part_units)
        for r in range(rows_dev // width_r):
            at = slice(r * width_r, (r + 1) * width_r)
            spread_grad = dot(d_hidden[rows, :], spread[:, at])
            d_pre = jnp.where(active[rows, at] > 0, spread_grad, 0.0).astype(jnp.bfloat16)
            product = dot(d_pre, feat_ref[at, :])
            if r == 0:
                total[...] = product
            else:
                total[...] += product
            if r % 2 == 1:
                advance(running)
        for q in range(part_units // LANES):
            launch(u * (part_units // LANES) + q, total[q * LANES : (q + 1) * LANES, :].T)
    while running:
        advance(running)
    for copy in started:
        copy.wait_send()


def fused(packed, labels, features, w_one, w_two, owner_steps):
    inner = split_axis("mlp", (2, None)) + split_axis("col", (2, None))
    own = split_axis("own", (None,))
    grad_steps = split_axis("col", (2, None)) + split_axis("own", (2, None))
    all_steps = inner + own
    rows_dev, width_f = features.shape
    units, classes = w_two.shape
    lists, list_rows, span = packed.shape
    sizes = lambda steps: [s[1] for s in steps]
    owners = 1
    for size in sizes(owner_steps):
        owners *= size
    groups = owners * list_rows
    targets = groups * GROUP
    chunks = own[0][1]
    bf16 = lambda *shape: pltpu.VMEM(shape, jnp.bfloat16)
    f32 = lambda *shape: pltpu.VMEM(shape, jnp.float32)

    def buffers(steps, pieces, outer, *block):
        held, recv = [], []
        for size in sizes(steps):
            outer //= size
            held.append(bf16(pieces, outer, size, *block))
            recv.append(bf16(pieces, size - 1, outer, *block))
        return held, recv

    own_rows = targets // chunks
    for size in sizes(inner):
        own_rows //= size
    pieces = (units + classes) // LANES
    grad_rows = width_f // owners
    held, recv = buffers(inner, chunks, targets // chunks // own_rows, own_rows, classes)
    own_held, own_recv = buffers(own, 1, chunks, own_rows, classes)
    grad_held, grad_recv = buffers(grad_steps, pieces, owners, grad_rows, LANES)

    def sems(steps, count):
        return [pltpu.SemaphoreType.DMA((count, s - 1)) for s in sizes(steps) for _ in range(2)]

    scratch = [
        f32(1, *reversed(sizes(owner_steps)), lists, list_rows, span),
        f32(groups, span), f32(groups, span), f32(groups, span),
        bf16(units, rows_dev), bf16(targets, rows_dev), bf16(units, targets), bf16(units, targets),
        f32(256, width_f),
        *held, *recv, *own_held, *own_recv,
        bf16(1, *reversed(sizes(all_steps)), own_rows, classes),
        *grad_held, *grad_recv,
        bf16(pieces, *reversed(sizes(grad_steps)), grad_rows, LANES),
        *sems(owner_steps, 1), *sems(inner, chunks), *sems(own, 1), *sems(all_steps, 1),
        *sems(grad_steps, pieces), *sems(grad_steps, pieces),
    ]
    vmem = pl.BlockSpec(memory_space=pltpu.VMEM)
    return pl.pallas_call(
        functools.partial(fused_kernel, (inner, own, owner_steps, grad_steps)),
        in_specs=[vmem] * 5,
        out_specs=[vmem] * 2,
        out_shape=[
            jax.ShapeDtypeStruct((width_f, units), jnp.bfloat16),
            jax.ShapeDtypeStruct((units, classes), jnp.bfloat16),
        ],
        scratch_shapes=scratch,
        compiler_params=pltpu.CompilerParams(
            collective_id=3, has_side_effects=True, vmem_limit_bytes=VMEM_LIMIT),
    )(packed, labels, features, w_one, w_two)


def body(features, nbr_page, nbr_weight, labels, w_one, w_two):
    own_axes = ("own", "col")
    units, classes = w_two.shape
    targets_dev, width_k = nbr_page.shape
    span = GROUP * width_k
    owner_steps = split_axis("col", (2, None)) + split_axis("own", (None,))
    all_steps = split_axis("mlp", (2, None)) + owner_steps
    owners = lax.axis_size(own_axes)
    if targets_dev * owners * features.shape[0] <= SPREAD_LIMIT:
        packed = jnp.stack([nbr_page.astype(jnp.float32), nbr_weight.astype(jnp.float32)])
        one, two = fused(packed.reshape(2, -1, span), labels[:, None], features, w_one, w_two, owner_steps)
        return one.astype(jnp.float32), two.astype(jnp.float32)
    pages, weights = gather_blocks(
        (nbr_page.reshape(-1, span), nbr_weight.reshape(-1, span)), owner_steps, 0)
    active_t, spread, hidden_t, part = forward(own_axes, pages, weights, features, w_one.T, w_two.T)
    dlog = sum_blocks(part, all_steps, 1, softmax_gradient, (labels[:, None],))
    grads = backward(dlog, hidden_t, w_two, spread, active_t, features)
    grads = sum_blocks(grads, owner_steps, 2).astype(jnp.float32)
    ones = units // LANES
    grad_one = jnp.concatenate([grads[p] for p in range(ones)], axis=1)
    grad_two = jnp.concatenate([grads[p] for p in range(ones, grads.shape[0])], axis=1)
    return grad_one, grad_two


def solution(mesh):
    placed = (
        P(("own", "col"), None),
        P(("own", "col"), None),
        P(("own", "col"), None),
        P(("own", "col")),
        P(None, "mlp"),
        P("mlp", None),
    )
    return jax.shard_map(
        body,
        mesh=mesh,
        in_specs=placed,
        out_specs=(P(None, "mlp"), P("mlp", None)),
        check_vma=False,
    )
```

```python
import functools
import jax
import jax.numpy as jnp
from jax import lax
from jax.experimental import pallas as pl
from jax.experimental.pallas import tpu as pltpu
from jax.sharding import PartitionSpec as P

GROUP = 8
LOW = 256
LANES = 128
SPREAD_LIMIT = 8 * 1024 * 1024
NT = (((1,), (1,)), ((), ()))
VMEM_LIMIT = 56 * 1024 * 1024


def dot(a, b):
    return jnp.dot(a, b, preferred_element_type=jnp.float32)


def dot_nt(a, b):
    return lax.dot_general(a, b, NT, preferred_element_type=jnp.float32)


MESH = pl.DeviceIdType.MESH


def split_axis(axis, parts):
    size = lax.axis_size(axis)
    steps, stride = [], 1
    for members in parts:
        members = size // stride if members is None else min(members, size // stride)
        if members > 1:
            steps.append((axis, members, stride))
        stride *= members
    return steps


def joined(steps):
    members = 1
    for step in steps:
        members *= step[1]
    return (tuple(steps), members, 0)


def place(step):
    axis, members, stride = step
    if stride:
        return lax.rem(lax.div(lax.axis_index(axis), stride), members)
    mine, weight = 0, 1
    for part in axis:
        mine = mine + place(part) * weight
        weight *= part[1]
    return mine


def partner(step, shift):
    axis, members, stride = step
    mine = place(step)
    other = lax.rem(mine + shift, members)
    if stride:
        return other, {axis: lax.axis_index(axis) + (other - mine) * stride}
    device, rest = {}, other
    for part in axis:
        device[part[0]] = lax.axis_index(part[0]) + (lax.rem(rest, part[1]) - place(part)) * part[2]
        rest = lax.div(rest, part[1])
    return other, device


def greet(steps):
    barrier = pltpu.get_barrier_semaphore()
    count = 0
    for step in steps:
        for shift in range(1, step[1]):
            pl.semaphore_signal(barrier, inc=1, device_id=partner(step, shift)[1], device_id_type=MESH)
            count += 1
    pl.semaphore_wait(barrier, count)


def start_scatter(step, piece, held, recv, sems, started):
    copies = []
    for shift in range(1, step[1]):
        other, device = partner(step, shift)
        copy = pltpu.make_async_remote_copy(
            src_ref=held.at[piece, :, other], dst_ref=recv.at[piece, shift - 1],
            send_sem=sems[0].at[piece, shift - 1], recv_sem=sems[1].at[piece, shift - 1],
            device_id=device, device_id_type=MESH)
        copy.start()
        copies.append(copy)
    started.extend(copies)
    return copies


def start_gather(steps, k, piece, full, sems, started):
    where = (piece,) + (slice(None),) * (len(steps) - 1 - k) + tuple(place(s) for s in reversed(steps[: k + 1]))
    copies = []
    for shift in range(1, steps[k][1]):
        copy = pltpu.make_async_remote_copy(
            src_ref=full.at[where], dst_ref=full.at[where],
            send_sem=sems[0].at[piece, shift - 1], recv_sem=sems[1].at[piece, shift - 1],
            device_id=partner(steps[k], shift)[1], device_id_type=MESH)
        copy.start()
        copies.append(copy)
    started.extend(copies)
    return copies


def settle(copies):
    for copy in copies:
        copy.wait_recv()


def sum_kernel(steps, pieces, finish, n_extra, *refs):
    first = refs[0]
    extra = refs[1 : 1 + n_extra]
    full = refs[1 + n_extra]
    scratch = refs[2 + n_extra :]
    count = len(steps)
    recv, held = scratch[:count], (first,) + scratch[count : 2 * count - 1]
    sems = scratch[2 * count - 1 :]
    scatter_sems = [(sems[2 * k], sems[2 * k + 1]) for k in range(count)]
    gather_sems = [(sems[2 * (count + k)], sems[2 * (count + k) + 1]) for k in range(count)]
    greet(steps)
    started = []
    flying = [start_scatter(steps[0], p, held[0], recv[0], scatter_sems[0], started) for p in range(pieces)]
    last = []
    for k in range(count):
        following = []
        for p in range(pieces):
            settle(flying[p])
            total = held[k][p, :, place(steps[k])].astype(jnp.float32)
            for j in range(steps[k][1] - 1):
                total = total + recv[k][p, j].astype(jnp.float32)
            if k + 1 < count:
                held[k + 1][p] = total.astype(jnp.bfloat16).reshape(held[k + 1].shape[1:])
                following.append(start_scatter(steps[k + 1], p, held[k + 1], recv[k + 1], scatter_sems[k + 1], started))
            else:
                last.append(total.reshape(total.shape[1:]))
                if finish is None:
                    full[(p,) + tuple(place(s) for s in reversed(steps))] = last[p].astype(jnp.bfloat16)
                    following.append(start_gather(steps, k, p, full, gather_sems[k], started))
        flying = following
    if finish is not None:
        results = finish(last, *extra)
        for p in range(pieces):
            full[(p,) + tuple(place(s) for s in reversed(steps))] = results[p].astype(jnp.bfloat16)
            flying.append(start_gather(steps, count - 1, p, full, gather_sems[count - 1], started))
    for k in range(count - 2, -1, -1):
        following = []
        for p in range(pieces):
            settle(flying[p])
            following.append(start_gather(steps, k, p, full, gather_sems[k], started))
        flying = following
    for p in range(pieces):
        settle(flying[p])
    for copy in started:
        copy.wait_send()


def sum_blocks(array, steps, collective_id, finish=None, extra=()):
    pieces, rows, lanes = array.shape
    sizes = [s[1] for s in steps]
    block = rows
    for size in sizes:
        block //= size
    recv, held, outer = [], [], rows // block
    for k, size in enumerate(sizes):
        outer //= size
        if k == 0:
            first = array.reshape(pieces, outer, size, block, lanes)
        else:
            held.append(pltpu.VMEM((pieces, outer, size, block, lanes), jnp.bfloat16))
        recv.append(pltpu.VMEM((pieces, size - 1, outer, block, lanes), jnp.bfloat16))
    sems = [pltpu.SemaphoreType.DMA((pieces, size - 1)) for size in sizes for _ in range(2)] * 2
    vmem = pl.BlockSpec(memory_space=pltpu.VMEM)
    full = pl.pallas_call(
        functools.partial(sum_kernel, steps, pieces, finish, len(extra)),
        in_specs=[vmem] * (1 + len(extra)),
        out_specs=vmem,
        out_shape=jax.ShapeDtypeStruct((pieces, *reversed(sizes), block, lanes), jnp.bfloat16),
        scratch_shapes=recv + held + sems,
        compiler_params=pltpu.CompilerParams(
            collective_id=collective_id, has_side_effects=True, vmem_limit_bytes=VMEM_LIMIT),
    )(first, *extra)
    return full.reshape(pieces, rows, lanes)


def gather_kernel(steps, *refs):
    count = len(refs) // 3
    ins, outs, sems = refs[:count], refs[count : 2 * count], refs[2 * count :]
    where = (0,) + tuple(place(s) for s in reversed(steps))
    greet(steps)
    started = []
    for a in range(count):
        outs[a][where] = ins[a][...]
    for k in range(len(steps) - 1, -1, -1):
        flying = []
        for a in range(count):
            pair = (sems[a].at[k, 0], sems[a].at[k, 1])
            flying.extend(start_gather(steps, k, 0, outs[a], pair, started))
        settle(flying)
    for copy in started:
        copy.wait_send()


def gather_blocks(arrays, steps, collective_id):
    sizes = [s[1] for s in steps]
    vmem = pl.BlockSpec(memory_space=pltpu.VMEM)
    outs = pl.pallas_call(
        functools.partial(gather_kernel, steps),
        in_specs=[vmem] * len(arrays),
        out_specs=[vmem] * len(arrays),
        out_shape=[jax.ShapeDtypeStruct((1, *reversed(sizes), *a.shape), a.dtype) for a in arrays],
        scratch_shapes=[pltpu.SemaphoreType.DMA((len(steps), 2, 1, max(sizes) - 1))] * len(arrays),
        compiler_params=pltpu.CompilerParams(
            collective_id=collective_id, has_side_effects=True, vmem_limit_bytes=VMEM_LIMIT),
    )(*arrays)
    return [o.reshape(-1, o.shape[-1]) for o in outs]


def softmax_gradient(logits, label_ref):
    lanes = logits[0].shape[1]
    rows = logits[0].shape[0]
    start = pl.multiple_of(lax.axis_index("mlp") * rows, rows)
    label = label_ref[pl.ds(start, rows), :]
    exponent = [jnp.exp(x) for x in logits]
    total = sum(jnp.sum(e, axis=1, keepdims=True) for e in exponent)
    results = []
    for p, e in enumerate(exponent):
        category = lax.broadcasted_iota(jnp.int32, e.shape, 1) + p * lanes
        results.append(e / total - jnp.where(category == label, 1.0, 0.0))
    return results


def build_spread(page_ref, weight_ref, first_row, rows_dev, spread_ref, chunk):
    span = page_ref.shape[1]
    width_k = span // GROUP
    high = rows_dev // LOW
    local = page_ref[...] - first_row
    here = (local >= 0) & (local < rows_dev)
    lane_target = lax.broadcasted_iota(jnp.int32, local.shape, 1) // width_k
    key = jnp.where(here, (local // LOW) * GROUP + lane_target, -1).astype(jnp.float32)
    low = jnp.where(here, local % LOW, -1).astype(jnp.float32)
    key = key.astype(jnp.bfloat16)
    low = low.astype(jnp.bfloat16)
    weight = weight_ref[...]
    zero = jnp.zeros((), jnp.bfloat16)
    one = jnp.ones((), jnp.bfloat16)
    key_rows = lax.broadcasted_iota(jnp.int32, (high * GROUP, span), 0).astype(jnp.float32).astype(jnp.bfloat16)
    low_rows = lax.broadcasted_iota(jnp.int32, (LOW, span), 0).astype(jnp.float32).astype(jnp.bfloat16)
    for pair in range(chunk // (2 * GROUP)):
        parts = []
        for g in (2 * pair, 2 * pair + 1):
            left = jnp.where(key_rows == key[g : g + 1, :], weight[g : g + 1, :], zero)
            right = jnp.where(low_rows == low[g : g + 1, :], one, zero)
            parts.append(dot_nt(left, right))
        for h in range(high):
            rows = [p[h * GROUP : (h + 1) * GROUP, :] for p in parts]
            spread_ref[2 * GROUP * pair : 2 * GROUP * (pair + 1), h * LOW : (h + 1) * LOW] = (
                jnp.concatenate(rows, axis=0).astype(jnp.bfloat16)
            )


def forward_kernel(own_axes, page_ref, weight_ref, feat_ref, w_one_t_ref, w_two_t_ref,
                   active_ref, spread_ref, hidden_ref, logit_ref):
    rows_dev = feat_ref.shape[0]
    chunk = spread_ref.shape[0]
    first_row = lax.axis_index(own_axes) * rows_dev

    @pl.when(pl.program_id(0) == 0)
    def _():
        def tile(i, _):
            at = pl.ds(pl.multiple_of(i * 512, 512), 512)
            pre = dot_nt(w_one_t_ref[...], feat_ref[at, :])
            active_ref[:, at] = jnp.maximum(pre, 0.0).astype(jnp.bfloat16)
            return 0
        lax.fori_loop(0, rows_dev // 512, tile, 0)

    build_spread(page_ref, weight_ref, first_row, rows_dev, spread_ref, chunk)
    hidden = dot_nt(active_ref[...], spread_ref[...]).astype(jnp.bfloat16)
    hidden_ref[...] = hidden
    logits = dot(w_two_t_ref[...], hidden).T.astype(jnp.bfloat16)
    lanes = logit_ref.shape[2]
    for p in range(logit_ref.shape[0]):
        logit_ref[p] = logits[:, p * lanes : (p + 1) * lanes]


def forward(own_axes, pages, weights, features, w_one_t, w_two_t):
    rows_dev, width_f = features.shape
    units = w_one_t.shape[0]
    classes = w_two_t.shape[0]
    groups, span = pages.shape
    targets = groups * GROUP
    chunk = min(256, targets)
    steps = targets // chunk
    whole = lambda shape: pl.BlockSpec(shape, lambda i: (0, 0))
    return pl.pallas_call(
        functools.partial(forward_kernel, own_axes),
        grid=(steps,),
        in_specs=[
            pl.BlockSpec((chunk // GROUP, span), lambda i: (i, 0)),
            pl.BlockSpec((chunk // GROUP, span), lambda i: (i, 0)),
            whole((rows_dev, width_f)),
            whole((units, width_f)),
            whole((classes, units)),
        ],
        out_specs=[
            whole((units, rows_dev)),
            pl.BlockSpec((chunk, rows_dev), lambda i: (i, 0)),
            pl.BlockSpec((units, chunk), lambda i: (0, i)),
            pl.BlockSpec((classes // LANES, chunk, LANES), lambda i: (0, i, 0)),
        ],
        out_shape=[
            jax.ShapeDtypeStruct((units, rows_dev), jnp.bfloat16),
            jax.ShapeDtypeStruct((targets, rows_dev), jnp.bfloat16),
            jax.ShapeDtypeStruct((units, targets), jnp.bfloat16),
            jax.ShapeDtypeStruct((classes // LANES, targets, LANES), jnp.bfloat16),
        ],
        compiler_params=pltpu.CompilerParams(vmem_limit_bytes=VMEM_LIMIT),
    )(pages, weights, features, w_one_t, w_two_t)


def backward_kernel(dlog_ref, hidden_ref, w_two_ref, spread_ref, active_ref, feat_ref,
                    grad_ref, d_hidden, total):
    step = pl.program_id(0)
    units = total.shape[0]
    width_f = total.shape[1]
    ones = units // LANES

    @pl.when(step == 0)
    def _():
        d_logits = jnp.concatenate([dlog_ref[p] for p in range(dlog_ref.shape[0])], axis=1)
        d_hidden[...] = dot_nt(w_two_ref[...], d_logits).astype(jnp.bfloat16)
        grad_two = dot(hidden_ref[...], d_logits).astype(jnp.bfloat16)
        for p in range(grad_two.shape[1] // LANES):
            grad_ref[ones + p] = grad_two[:, p * LANES : (p + 1) * LANES]
        total[...] = jnp.zeros_like(total)

    spread_grad = dot(d_hidden[...], spread_ref[...])
    d_pre = jnp.where(active_ref[...] > 0, spread_grad, 0.0).astype(jnp.bfloat16)
    total[...] += dot(d_pre, feat_ref[...])

    @pl.when(step == pl.num_programs(0) - 1)
    def _():
        for p in range(ones):
            grad_ref[p] = total[p * LANES : (p + 1) * LANES, :].T.astype(jnp.bfloat16)


def backward(dlog, hidden_t, w_two, spread, active_t, features):
    rows_dev, width_f = features.shape
    units, classes = w_two.shape
    assert units == width_f
    targets = spread.shape[0]
    block = 512
    whole = lambda shape: pl.BlockSpec(shape, lambda i: (0,) * len(shape))
    out = ((units + classes) // LANES, width_f, LANES)
    return pl.pallas_call(
        backward_kernel,
        grid=(rows_dev // block,),
        in_specs=[
            whole(dlog.shape),
            whole((units, targets)),
            whole((units, classes)),
            pl.BlockSpec((targets, block), lambda i: (0, i)),
            pl.BlockSpec((units, block), lambda i: (0, i)),
            pl.BlockSpec((block, width_f), lambda i: (i, 0)),
        ],
        out_specs=whole(out),
        out_shape=jax.ShapeDtypeStruct(out, jnp.bfloat16),
        scratch_shapes=[
            pltpu.VMEM((units, targets), jnp.bfloat16),
            pltpu.VMEM((units, width_f), jnp.float32),
        ],
        compiler_params=pltpu.CompilerParams(vmem_limit_bytes=VMEM_LIMIT),
    )(dlog, hidden_t, w_two, spread, active_t, features)


def scatter_total(step, piece, held, recv):
    total = held[piece, :, place(step)].astype(jnp.float32)
    for j in range(step[1] - 1):
        total = total + recv[piece, j].astype(jnp.float32)
    return total


def advance(running):
    for task in list(running):
        if next(task, "done") == "done":
            running.remove(task)


def fused_kernel(plan, *refs):
    it = iter(refs)
    page_ref, weight_ref, label_ref, feat_ref, w_one_ref, w_two_ref, one_ref, two_ref = (next(it) for _ in range(8))
    loose, pages_all, key_s, low_s, weight_s, active, spread, hidden, d_hidden, total = (next(it) for _ in range(10))
    inner, own, owner_steps, grad_steps = plan
    all_steps = inner + own
    low_step, high_step = split_axis("mlp", (2, None))
    chunks = lax.axis_size("own")
    held = [next(it) for _ in inner]
    recv = [next(it) for _ in inner]
    own_held, own_recv, full = (next(it) for _ in range(3))
    grad_held = [next(it) for _ in grad_steps]
    grad_recv = [next(it) for _ in grad_steps]
    grad_full = next(it)
    pairs = lambda n: [(next(it), next(it)) for _ in range(n)]
    page_sems = pairs(len(owner_steps))
    inner_sems = pairs(len(inner))
    own_sems = pairs(1)[0]
    land_sems, cross_sems, core_sems = pairs(3)
    scatter_sems = pairs(len(grad_steps))
    gather_sems = pairs(len(grad_steps))

    rows_dev, width_f = feat_ref.shape
    units, classes = w_two_ref.shape
    targets = spread.shape[0]
    chunk = targets // chunks
    span = key_s.shape[1]
    width_k = span // GROUP
    high = rows_dev // LOW
    started = []

    greet(all_steps)
    ids = page_ref[...]
    loose[0] = (ids // LOW).astype(jnp.float32)
    loose[1] = (ids % LOW).astype(jnp.float32)
    loose[2] = weight_ref[...].astype(jnp.float32)
    count = ids.shape[0] // GROUP
    lists = [
        jnp.concatenate([loose[a, pl.ds(j, count, stride=GROUP), :] for j in range(GROUP)], axis=1)
        for a in range(3)
    ]
    pages_all[(0,) + tuple(place(s) for s in reversed(owner_steps))] = jnp.stack(lists).astype(jnp.bfloat16)
    w_one_t = w_one_ref[...].T
    stages = len(owner_steps)
    tiles = rows_dev // 512
    for k in range(stages - 1, -1, -1):
        flying = start_gather(owner_steps, k, 0, pages_all, page_sems[k], started)
        done = stages - 1 - k
        for i in range(done * tiles // stages, (done + 1) * tiles // stages):
            pre = dot_nt(w_one_t, feat_ref[i * 512 : (i + 1) * 512, :])
            active[:, i * 512 : (i + 1) * 512] = jnp.maximum(pre, 0.0).astype(jnp.bfloat16)
        settle(flying)

    lists = pages_all[0].astype(jnp.float32)
    lead = (slice(None),) * stages
    local = lists[lead + (0,)].reshape(-1, span) - (lax.axis_index(("own", "col")) * high).astype(jnp.float32)
    here = (local >= 0) & (local < high)
    lane_target = (lax.broadcasted_iota(jnp.int32, local.shape, 1) // width_k).astype(jnp.float32)
    key_s[...] = jnp.where(here, local * GROUP + lane_target, -1.0)
    low_s[...] = lists[lead + (1,)].reshape(-1, span)
    weight_s[...] = lists[lead + (2,)].reshape(-1, span)

    zero = jnp.zeros((), jnp.bfloat16)
    one = jnp.ones((), jnp.bfloat16)
    key_rows = lax.broadcasted_iota(jnp.int32, (high * GROUP, span), 0).astype(jnp.float32).astype(jnp.bfloat16)
    low_rows = lax.broadcasted_iota(jnp.int32, (LOW, span), 0).astype(jnp.float32).astype(jnp.bfloat16)

    def build(i, carry):
        at = pl.ds(pl.multiple_of(i * 8, 8), 8)
        key = key_s[at, :].astype(jnp.bfloat16)
        low = low_s[at, :].astype(jnp.bfloat16)
        weight = weight_s[at, :].astype(jnp.bfloat16)
        for pair in range(4):
            parts = []
            for g in (2 * pair, 2 * pair + 1):
                left = jnp.where(key_rows == key[g : g + 1, :], weight[g : g + 1, :], zero)
                right = jnp.where(low_rows == low[g : g + 1, :], one, zero)
                parts.append(dot_nt(left, right))
            rows = pl.ds(pl.multiple_of(i * 64 + pair * 16, 16), 16)
            for h in range(high):
                both = [p[h * GROUP : (h + 1) * GROUP, :] for p in parts]
                spread[rows, h * LOW : (h + 1) * LOW] = jnp.concatenate(both, axis=0).astype(jnp.bfloat16)
        return carry

    def sum_logits(c):
        for k, step in enumerate(inner):
            copies = start_scatter(step, c, held[k], recv[k], inner_sems[k], started)
            yield
            settle(copies)
            part = scatter_total(step, c, held[k], recv[k]).astype(jnp.bfloat16)
            if k + 1 < len(inner):
                held[k + 1][c] = part.reshape(held[k + 1].shape[1:])
            else:
                each = own[0][1] // chunks
                own_held[0, 0, c * each : (c + 1) * each] = part

    running = []
    w_two_t = w_two_ref[...].T
    blocks = chunk // 64
    for c in range(chunks):
        half = blocks // 2
        lax.fori_loop(c * blocks, c * blocks + half, build, 0)
        advance(running)
        lax.fori_loop(c * blocks + half, (c + 1) * blocks, build, 0)
        advance(running)
        block = dot_nt(active[...], spread[c * chunk : (c + 1) * chunk, :]).astype(jnp.bfloat16)
        hidden[:, c * chunk : (c + 1) * chunk] = block
        held[0][c] = dot(w_two_t, block).T.astype(jnp.bfloat16).reshape(held[0].shape[1:])
        advance(running)
        running.append(sum_logits(c))
        next(running[-1])
    while running:
        advance(running)
    settle(start_scatter(own[0], 0, own_held, own_recv, own_sems, started))
    logits = scatter_total(own[0], 0, own_held, own_recv)[0]
    rows = logits.shape[0]
    at_label = lax.broadcasted_iota(jnp.int32, (rows, label_ref.shape[1]), 0) + lax.axis_index("mlp") * rows
    lane = lax.broadcasted_iota(jnp.int32, at_label.shape, 1)
    label = jnp.sum(jnp.where(lane == at_label, label_ref[...].astype(jnp.float32), 0.0), axis=1, keepdims=True)
    exponent = jnp.exp(logits)
    category = lax.broadcasted_iota(jnp.int32, logits.shape, 1).astype(jnp.float32)
    probability = exponent / jnp.sum(exponent, axis=1, keepdims=True)
    d_logits = (probability - jnp.where(category == label, 1.0, 0.0)).astype(jnp.bfloat16)

    owner, upper, lower = place(own[0]), place(high_step), place(low_step)
    full[0, owner, upper, lower] = d_logits

    def send(where, sems, at, device):
        copy = pltpu.make_async_remote_copy(
            src_ref=full.at[where], dst_ref=full.at[where], send_sem=sems[0].at[at], recv_sem=sems[1].at[at],
            device_id=device, device_id_type=MESH)
        copy.start()
        started.append(copy)
        return copy

    members = own[0][1]
    landing = [
        send((0, owner, upper, lower), land_sems, (shift - 1,), partner(own[0], shift)[1])
        for shift in range(1, members)
    ]
    crossing = []
    for shift in range(members):
        if shift:
            landing[shift - 1].wait_recv()
        origin = lax.rem(owner + members - shift, members)
        for hop in range(1, high_step[1]):
            crossing.append(send(
                (0, origin, upper, lower), cross_sems, (shift, hop - 1), partner(high_step, hop)[1]))
    other_core = partner(low_step, 1)[1]
    final = [send((0, slice(None), upper, lower), core_sems, (0,), other_core)]
    settle(crossing)
    for hop in range(1, high_step[1]):
        origin = lax.rem(upper + high_step[1] - hop, high_step[1])
        final.append(send((0, slice(None), origin, lower), core_sems, (hop,), other_core))
    settle(final)
    d_logits = full[0].reshape(targets, classes)

    def sum_grads(p, values):
        grad_held[0][p] = values.astype(jnp.bfloat16).reshape(grad_held[0].shape[1:])
        count = len(grad_steps)
        for k, step in enumerate(grad_steps):
            copies = start_scatter(step, p, grad_held[k], grad_recv[k], scatter_sems[k], started)
            yield
            settle(copies)
            part = scatter_total(step, p, grad_held[k], grad_recv[k]).astype(jnp.bfloat16)
            if k + 1 < count:
                grad_held[k + 1][p] = part.reshape(grad_held[k + 1].shape[1:])
        grad_full[(p,) + tuple(place(s) for s in reversed(grad_steps))] = part[0]
        for k in range(count - 1, -1, -1):
            copies = start_gather(grad_steps, k, p, grad_full, gather_sems[k], started)
            yield
            settle(copies)
        block = grad_full[p].reshape(width_f, LANES)
        if p < units // LANES:
            one_ref[:, p * LANES : (p + 1) * LANES] = block
        else:
            q = p - units // LANES
            two_ref[:, q * LANES : (q + 1) * LANES] = block

    def launch(p, values):
        running.append(sum_grads(p, values))
        next(running[-1])

    grad_two = dot(hidden[...], d_logits)
    for q in range(classes // LANES):
        launch(units // LANES + q, grad_two[:, q * LANES : (q + 1) * LANES])
    d_hidden[...] = dot_nt(w_two_ref[...], d_logits).astype(jnp.bfloat16)
    part_units = 256
    width_r = 1024
    for u in range(units // part_units):
        rows = slice(u * part_units, (u + 1) * part_units)
        for r in range(rows_dev // width_r):
            at = slice(r * width_r, (r + 1) * width_r)
            spread_grad = dot(d_hidden[rows, :], spread[:, at])
            d_pre = jnp.where(active[rows, at] > 0, spread_grad, 0.0).astype(jnp.bfloat16)
            product = dot(d_pre, feat_ref[at, :])
            if r == 0:
                total[...] = product
            else:
                total[...] += product
            advance(running)
        for q in range(part_units // LANES):
            launch(u * (part_units // LANES) + q, total[q * LANES : (q + 1) * LANES, :].T)
    while running:
        advance(running)
    for copy in started:
        copy.wait_send()


def fused(nbr_page, nbr_weight, labels, features, w_one, w_two, owner_steps):
    inner = split_axis("mlp", (None,))
    own = [joined(owner_steps)]
    grad_steps = owner_steps
    all_steps = inner + own
    rows_dev, width_f = features.shape
    units, classes = w_two.shape
    lists, list_rows, span = 3, nbr_page.shape[0] // GROUP, GROUP * nbr_page.shape[1]
    sizes = lambda steps: [s[1] for s in steps]
    owners = 1
    for size in sizes(owner_steps):
        owners *= size
    groups = owners * list_rows
    targets = groups * GROUP
    chunks = lax.axis_size("own")
    bf16 = lambda *shape: pltpu.VMEM(shape, jnp.bfloat16)
    f32 = lambda *shape: pltpu.VMEM(shape, jnp.float32)

    def buffers(steps, pieces, outer, *block):
        held, recv = [], []
        for size in sizes(steps):
            outer //= size
            held.append(bf16(pieces, outer, size, *block))
            recv.append(bf16(pieces, size - 1, outer, *block))
        return held, recv

    own_rows = targets // owners
    for size in sizes(inner):
        own_rows //= size
    upper = lax.axis_size("mlp") // 2
    pieces = (units + classes) // LANES
    grad_rows = width_f // owners
    held, recv = buffers(inner, chunks, targets // chunks // own_rows, own_rows, classes)
    own_held, own_recv = buffers(own, 1, owners, own_rows, classes)
    grad_held, grad_recv = buffers(grad_steps, pieces, owners, grad_rows, LANES)

    def sems(steps, count):
        return [pltpu.SemaphoreType.DMA((count, s - 1)) for s in sizes(steps) for _ in range(2)]

    scratch = [
        f32(lists, *nbr_page.shape), bf16(1, *reversed(sizes(owner_steps)), lists, list_rows, span),
        f32(groups, span), f32(groups, span), f32(groups, span),
        bf16(units, rows_dev), bf16(targets, rows_dev), bf16(units, targets), bf16(units, targets),
        f32(256, width_f),
        *held, *recv, *own_held, *own_recv,
        bf16(1, owners, upper, 2, own_rows, classes),
        *grad_held, *grad_recv,
        bf16(pieces, *reversed(sizes(grad_steps)), grad_rows, LANES),
        *sems(owner_steps, 1), *sems(inner, chunks), *sems(own, 1),
        *[pltpu.SemaphoreType.DMA(shape) for shape in ((owners - 1,), (owners, upper - 1), (upper,)) for _ in range(2)],
        *sems(grad_steps, pieces), *sems(grad_steps, pieces),
    ]
    vmem = pl.BlockSpec(memory_space=pltpu.VMEM)
    return pl.pallas_call(
        functools.partial(fused_kernel, (inner, own, owner_steps, grad_steps)),
        in_specs=[vmem] * 6,
        out_specs=[vmem] * 2,
        out_shape=[
            jax.ShapeDtypeStruct((width_f, units), jnp.bfloat16),
            jax.ShapeDtypeStruct((units, classes), jnp.bfloat16),
        ],
        scratch_shapes=scratch,
        compiler_params=pltpu.CompilerParams(
            collective_id=3, has_side_effects=True, vmem_limit_bytes=VMEM_LIMIT),
    )(nbr_page, nbr_weight, labels.reshape(1, -1), features, w_one, w_two)


def body(features, nbr_page, nbr_weight, labels, w_one, w_two):
    own_axes = ("own", "col")
    units, classes = w_two.shape
    targets_dev, width_k = nbr_page.shape
    span = GROUP * width_k
    owner_steps = split_axis("col", (2, None)) + split_axis("own", (None,))
    all_steps = split_axis("mlp", (2, None)) + owner_steps
    owners = lax.axis_size(own_axes)
    small = targets_dev * owners * features.shape[0] <= SPREAD_LIMIT
    if small and owners * features.shape[0] <= LOW * LOW and lax.axis_size("mlp") >= 4:
        one, two = fused(nbr_page, nbr_weight, labels, features, w_one, w_two, owner_steps)
        return one.astype(jnp.float32), two.astype(jnp.float32)
    pages, weights = gather_blocks(
        (nbr_page.reshape(-1, span), nbr_weight.reshape(-1, span)), owner_steps, 0)
    active_t, spread, hidden_t, part = forward(own_axes, pages, weights, features, w_one.T, w_two.T)
    dlog = sum_blocks(part, all_steps, 1, softmax_gradient, (labels[:, None],))
    grads = backward(dlog, hidden_t, w_two, spread, active_t, features)
    grads = sum_blocks(grads, owner_steps, 2).astype(jnp.float32)
    ones = units // LANES
    grad_one = jnp.concatenate([grads[p] for p in range(ones)], axis=1)
    grad_two = jnp.concatenate([grads[p] for p in range(ones, grads.shape[0])], axis=1)
    return grad_one, grad_two


def solution(mesh):
    placed = (
        P(("own", "col"), None),
        P(("own", "col"), None),
        P(("own", "col"), None),
        P(("own", "col")),
        P(None, "mlp"),
        P("mlp", None),
    )
    return jax.shard_map(
        body,
        mesh=mesh,
        in_specs=placed,
        out_specs=(P(None, "mlp"), P("mlp", None)),
        check_vma=False,
    )
```

```python
import functools
import jax
import jax.numpy as jnp
from jax import lax
from jax.experimental import pallas as pl
from jax.experimental.pallas import tpu as pltpu
from jax.sharding import PartitionSpec as P

GROUP = 8
LOW = 256
LANES = 128
SPREAD_LIMIT = 8 * 1024 * 1024
NT = (((1,), (1,)), ((), ()))
VMEM_LIMIT = 56 * 1024 * 1024


def dot(a, b):
    return jnp.dot(a, b, preferred_element_type=jnp.float32)


def dot_nt(a, b):
    return lax.dot_general(a, b, NT, preferred_element_type=jnp.float32)


MESH = pl.DeviceIdType.MESH


def split_axis(axis, parts):
    size = lax.axis_size(axis)
    steps, stride = [], 1
    for members in parts:
        members = size // stride if members is None else min(members, size // stride)
        if members > 1:
            steps.append((axis, members, stride))
        stride *= members
    return steps


def joined(steps):
    members = 1
    for step in steps:
        members *= step[1]
    return (tuple(steps), members, 0)


def place(step):
    axis, members, stride = step
    if stride:
        return lax.rem(lax.div(lax.axis_index(axis), stride), members)
    mine, weight = 0, 1
    for part in axis:
        mine = mine + place(part) * weight
        weight *= part[1]
    return mine


def partner(step, shift):
    axis, members, stride = step
    mine = place(step)
    other = lax.rem(mine + shift, members)
    if stride:
        return other, {axis: lax.axis_index(axis) + (other - mine) * stride}
    device, rest = {}, other
    for part in axis:
        device[part[0]] = lax.axis_index(part[0]) + (lax.rem(rest, part[1]) - place(part)) * part[2]
        rest = lax.div(rest, part[1])
    return other, device


def greet(steps):
    barrier = pltpu.get_barrier_semaphore()
    count = 0
    for step in steps:
        for shift in range(1, step[1]):
            pl.semaphore_signal(barrier, inc=1, device_id=partner(step, shift)[1], device_id_type=MESH)
            count += 1
    pl.semaphore_wait(barrier, count)


def start_scatter(step, piece, held, recv, sems, started):
    copies = []
    for shift in range(1, step[1]):
        other, device = partner(step, shift)
        copy = pltpu.make_async_remote_copy(
            src_ref=held.at[piece, :, other], dst_ref=recv.at[piece, shift - 1],
            send_sem=sems[0].at[piece, shift - 1], recv_sem=sems[1].at[piece, shift - 1],
            device_id=device, device_id_type=MESH)
        copy.start()
        copies.append(copy)
    started.extend(copies)
    return copies


def start_gather(steps, k, piece, full, sems, started):
    where = (piece,) + (slice(None),) * (len(steps) - 1 - k) + tuple(place(s) for s in reversed(steps[: k + 1]))
    copies = []
    for shift in range(1, steps[k][1]):
        copy = pltpu.make_async_remote_copy(
            src_ref=full.at[where], dst_ref=full.at[where],
            send_sem=sems[0].at[piece, shift - 1], recv_sem=sems[1].at[piece, shift - 1],
            device_id=partner(steps[k], shift)[1], device_id_type=MESH)
        copy.start()
        copies.append(copy)
    started.extend(copies)
    return copies


def settle(copies):
    for copy in copies:
        copy.wait_recv()


def sum_kernel(steps, pieces, finish, n_extra, *refs):
    first = refs[0]
    extra = refs[1 : 1 + n_extra]
    full = refs[1 + n_extra]
    scratch = refs[2 + n_extra :]
    count = len(steps)
    recv, held = scratch[:count], (first,) + scratch[count : 2 * count - 1]
    sems = scratch[2 * count - 1 :]
    scatter_sems = [(sems[2 * k], sems[2 * k + 1]) for k in range(count)]
    gather_sems = [(sems[2 * (count + k)], sems[2 * (count + k) + 1]) for k in range(count)]
    greet(steps)
    started = []
    flying = [start_scatter(steps[0], p, held[0], recv[0], scatter_sems[0], started) for p in range(pieces)]
    last = []
    for k in range(count):
        following = []
        for p in range(pieces):
            settle(flying[p])
            total = held[k][p, :, place(steps[k])].astype(jnp.float32)
            for j in range(steps[k][1] - 1):
                total = total + recv[k][p, j].astype(jnp.float32)
            if k + 1 < count:
                held[k + 1][p] = total.astype(jnp.bfloat16).reshape(held[k + 1].shape[1:])
                following.append(start_scatter(steps[k + 1], p, held[k + 1], recv[k + 1], scatter_sems[k + 1], started))
            else:
                last.append(total.reshape(total.shape[1:]))
                if finish is None:
                    full[(p,) + tuple(place(s) for s in reversed(steps))] = last[p].astype(jnp.bfloat16)
                    following.append(start_gather(steps, k, p, full, gather_sems[k], started))
        flying = following
    if finish is not None:
        results = finish(last, *extra)
        for p in range(pieces):
            full[(p,) + tuple(place(s) for s in reversed(steps))] = results[p].astype(jnp.bfloat16)
            flying.append(start_gather(steps, count - 1, p, full, gather_sems[count - 1], started))
    for k in range(count - 2, -1, -1):
        following = []
        for p in range(pieces):
            settle(flying[p])
            following.append(start_gather(steps, k, p, full, gather_sems[k], started))
        flying = following
    for p in range(pieces):
        settle(flying[p])
    for copy in started:
        copy.wait_send()


def sum_blocks(array, steps, collective_id, finish=None, extra=()):
    pieces, rows, lanes = array.shape
    sizes = [s[1] for s in steps]
    block = rows
    for size in sizes:
        block //= size
    recv, held, outer = [], [], rows // block
    for k, size in enumerate(sizes):
        outer //= size
        if k == 0:
            first = array.reshape(pieces, outer, size, block, lanes)
        else:
            held.append(pltpu.VMEM((pieces, outer, size, block, lanes), jnp.bfloat16))
        recv.append(pltpu.VMEM((pieces, size - 1, outer, block, lanes), jnp.bfloat16))
    sems = [pltpu.SemaphoreType.DMA((pieces, size - 1)) for size in sizes for _ in range(2)] * 2
    vmem = pl.BlockSpec(memory_space=pltpu.VMEM)
    full = pl.pallas_call(
        functools.partial(sum_kernel, steps, pieces, finish, len(extra)),
        in_specs=[vmem] * (1 + len(extra)),
        out_specs=vmem,
        out_shape=jax.ShapeDtypeStruct((pieces, *reversed(sizes), block, lanes), jnp.bfloat16),
        scratch_shapes=recv + held + sems,
        compiler_params=pltpu.CompilerParams(
            collective_id=collective_id, has_side_effects=True, vmem_limit_bytes=VMEM_LIMIT),
    )(first, *extra)
    return full.reshape(pieces, rows, lanes)


def gather_kernel(steps, *refs):
    count = len(refs) // 3
    ins, outs, sems = refs[:count], refs[count : 2 * count], refs[2 * count :]
    where = (0,) + tuple(place(s) for s in reversed(steps))
    greet(steps)
    started = []
    for a in range(count):
        outs[a][where] = ins[a][...]
    for k in range(len(steps) - 1, -1, -1):
        flying = []
        for a in range(count):
            pair = (sems[a].at[k, 0], sems[a].at[k, 1])
            flying.extend(start_gather(steps, k, 0, outs[a], pair, started))
        settle(flying)
    for copy in started:
        copy.wait_send()


def gather_blocks(arrays, steps, collective_id):
    sizes = [s[1] for s in steps]
    vmem = pl.BlockSpec(memory_space=pltpu.VMEM)
    outs = pl.pallas_call(
        functools.partial(gather_kernel, steps),
        in_specs=[vmem] * len(arrays),
        out_specs=[vmem] * len(arrays),
        out_shape=[jax.ShapeDtypeStruct((1, *reversed(sizes), *a.shape), a.dtype) for a in arrays],
        scratch_shapes=[pltpu.SemaphoreType.DMA((len(steps), 2, 1, max(sizes) - 1))] * len(arrays),
        compiler_params=pltpu.CompilerParams(
            collective_id=collective_id, has_side_effects=True, vmem_limit_bytes=VMEM_LIMIT),
    )(*arrays)
    return [o.reshape(-1, o.shape[-1]) for o in outs]


def softmax_gradient(logits, label_ref):
    lanes = logits[0].shape[1]
    rows = logits[0].shape[0]
    start = pl.multiple_of(lax.axis_index("mlp") * rows, rows)
    label = label_ref[pl.ds(start, rows), :]
    exponent = [jnp.exp(x) for x in logits]
    total = sum(jnp.sum(e, axis=1, keepdims=True) for e in exponent)
    results = []
    for p, e in enumerate(exponent):
        category = lax.broadcasted_iota(jnp.int32, e.shape, 1) + p * lanes
        results.append(e / total - jnp.where(category == label, 1.0, 0.0))
    return results


def build_spread(page_ref, weight_ref, first_row, rows_dev, spread_ref, chunk):
    span = page_ref.shape[1]
    width_k = span // GROUP
    high = rows_dev // LOW
    local = page_ref[...] - first_row
    here = (local >= 0) & (local < rows_dev)
    lane_target = lax.broadcasted_iota(jnp.int32, local.shape, 1) // width_k
    key = jnp.where(here, (local // LOW) * GROUP + lane_target, -1).astype(jnp.float32)
    low = jnp.where(here, local % LOW, -1).astype(jnp.float32)
    key = key.astype(jnp.bfloat16)
    low = low.astype(jnp.bfloat16)
    weight = weight_ref[...]
    zero = jnp.zeros((), jnp.bfloat16)
    one = jnp.ones((), jnp.bfloat16)
    key_rows = lax.broadcasted_iota(jnp.int32, (high * GROUP, span), 0).astype(jnp.float32).astype(jnp.bfloat16)
    low_rows = lax.broadcasted_iota(jnp.int32, (LOW, span), 0).astype(jnp.float32).astype(jnp.bfloat16)
    for pair in range(chunk // (2 * GROUP)):
        parts = []
        for g in (2 * pair, 2 * pair + 1):
            left = jnp.where(key_rows == key[g : g + 1, :], weight[g : g + 1, :], zero)
            right = jnp.where(low_rows == low[g : g + 1, :], one, zero)
            parts.append(dot_nt(left, right))
        for h in range(high):
            rows = [p[h * GROUP : (h + 1) * GROUP, :] for p in parts]
            spread_ref[2 * GROUP * pair : 2 * GROUP * (pair + 1), h * LOW : (h + 1) * LOW] = (
                jnp.concatenate(rows, axis=0).astype(jnp.bfloat16)
            )


def forward_kernel(own_axes, page_ref, weight_ref, feat_ref, w_one_t_ref, w_two_t_ref,
                   active_ref, spread_ref, hidden_ref, logit_ref):
    rows_dev = feat_ref.shape[0]
    chunk = spread_ref.shape[0]
    first_row = lax.axis_index(own_axes) * rows_dev

    @pl.when(pl.program_id(0) == 0)
    def _():
        def tile(i, _):
            at = pl.ds(pl.multiple_of(i * 512, 512), 512)
            pre = dot_nt(w_one_t_ref[...], feat_ref[at, :])
            active_ref[:, at] = jnp.maximum(pre, 0.0).astype(jnp.bfloat16)
            return 0
        lax.fori_loop(0, rows_dev // 512, tile, 0)

    build_spread(page_ref, weight_ref, first_row, rows_dev, spread_ref, chunk)
    hidden = dot_nt(active_ref[...], spread_ref[...]).astype(jnp.bfloat16)
    hidden_ref[...] = hidden
    logits = dot(w_two_t_ref[...], hidden).T.astype(jnp.bfloat16)
    lanes = logit_ref.shape[2]
    for p in range(logit_ref.shape[0]):
        logit_ref[p] = logits[:, p * lanes : (p + 1) * lanes]


def forward(own_axes, pages, weights, features, w_one_t, w_two_t):
    rows_dev, width_f = features.shape
    units = w_one_t.shape[0]
    classes = w_two_t.shape[0]
    groups, span = pages.shape
    targets = groups * GROUP
    chunk = min(256, targets)
    steps = targets // chunk
    whole = lambda shape: pl.BlockSpec(shape, lambda i: (0, 0))
    return pl.pallas_call(
        functools.partial(forward_kernel, own_axes),
        grid=(steps,),
        in_specs=[
            pl.BlockSpec((chunk // GROUP, span), lambda i: (i, 0)),
            pl.BlockSpec((chunk // GROUP, span), lambda i: (i, 0)),
            whole((rows_dev, width_f)),
            whole((units, width_f)),
            whole((classes, units)),
        ],
        out_specs=[
            whole((units, rows_dev)),
            pl.BlockSpec((chunk, rows_dev), lambda i: (i, 0)),
            pl.BlockSpec((units, chunk), lambda i: (0, i)),
            pl.BlockSpec((classes // LANES, chunk, LANES), lambda i: (0, i, 0)),
        ],
        out_shape=[
            jax.ShapeDtypeStruct((units, rows_dev), jnp.bfloat16),
            jax.ShapeDtypeStruct((targets, rows_dev), jnp.bfloat16),
            jax.ShapeDtypeStruct((units, targets), jnp.bfloat16),
            jax.ShapeDtypeStruct((classes // LANES, targets, LANES), jnp.bfloat16),
        ],
        compiler_params=pltpu.CompilerParams(vmem_limit_bytes=VMEM_LIMIT),
    )(pages, weights, features, w_one_t, w_two_t)


def backward_kernel(dlog_ref, hidden_ref, w_two_ref, spread_ref, active_ref, feat_ref,
                    grad_ref, d_hidden, total):
    step = pl.program_id(0)
    units = total.shape[0]
    width_f = total.shape[1]
    ones = units // LANES

    @pl.when(step == 0)
    def _():
        d_logits = jnp.concatenate([dlog_ref[p] for p in range(dlog_ref.shape[0])], axis=1)
        d_hidden[...] = dot_nt(w_two_ref[...], d_logits).astype(jnp.bfloat16)
        grad_two = dot(hidden_ref[...], d_logits).astype(jnp.bfloat16)
        for p in range(grad_two.shape[1] // LANES):
            grad_ref[ones + p] = grad_two[:, p * LANES : (p + 1) * LANES]
        total[...] = jnp.zeros_like(total)

    spread_grad = dot(d_hidden[...], spread_ref[...])
    d_pre = jnp.where(active_ref[...] > 0, spread_grad, 0.0).astype(jnp.bfloat16)
    total[...] += dot(d_pre, feat_ref[...])

    @pl.when(step == pl.num_programs(0) - 1)
    def _():
        for p in range(ones):
            grad_ref[p] = total[p * LANES : (p + 1) * LANES, :].T.astype(jnp.bfloat16)


def backward(dlog, hidden_t, w_two, spread, active_t, features):
    rows_dev, width_f = features.shape
    units, classes = w_two.shape
    assert units == width_f
    targets = spread.shape[0]
    block = 512
    whole = lambda shape: pl.BlockSpec(shape, lambda i: (0,) * len(shape))
    out = ((units + classes) // LANES, width_f, LANES)
    return pl.pallas_call(
        backward_kernel,
        grid=(rows_dev // block,),
        in_specs=[
            whole(dlog.shape),
            whole((units, targets)),
            whole((units, classes)),
            pl.BlockSpec((targets, block), lambda i: (0, i)),
            pl.BlockSpec((units, block), lambda i: (0, i)),
            pl.BlockSpec((block, width_f), lambda i: (i, 0)),
        ],
        out_specs=whole(out),
        out_shape=jax.ShapeDtypeStruct(out, jnp.bfloat16),
        scratch_shapes=[
            pltpu.VMEM((units, targets), jnp.bfloat16),
            pltpu.VMEM((units, width_f), jnp.float32),
        ],
        compiler_params=pltpu.CompilerParams(vmem_limit_bytes=VMEM_LIMIT),
    )(dlog, hidden_t, w_two, spread, active_t, features)


def scatter_total(step, piece, held, recv):
    total = held[piece, :, place(step)].astype(jnp.float32)
    for j in range(step[1] - 1):
        total = total + recv[piece, j].astype(jnp.float32)
    return total


def advance(running):
    for task in list(running):
        if next(task, "done") == "done":
            running.remove(task)


def fused_kernel(plan, *refs):
    it = iter(refs)
    page_ref, weight_ref, label_ref, feat_ref, w_one_ref, w_two_ref, one_ref, two_ref = (next(it) for _ in range(8))
    loose, pages_all, key_s, low_s, weight_s, active, active_t, spread, hidden, d_hidden, total = (next(it) for _ in range(11))
    inner, own, owner_steps, grad_steps = plan
    all_steps = inner + own
    low_step, high_step = split_axis("mlp", (2, None))
    chunks = lax.axis_size("own")
    held = [next(it) for _ in inner]
    recv = [next(it) for _ in inner]
    own_held, own_recv, full = (next(it) for _ in range(3))
    grad_held = [next(it) for _ in grad_steps]
    grad_recv = [next(it) for _ in grad_steps]
    grad_full = next(it)
    pairs = lambda n: [(next(it), next(it)) for _ in range(n)]
    page_sems = pairs(len(owner_steps))
    inner_sems = pairs(len(inner))
    own_sems = pairs(1)[0]
    land_sems, cross_sems, core_sems = pairs(3)
    scatter_sems = pairs(len(grad_steps))
    gather_sems = pairs(len(grad_steps))

    rows_dev, width_f = feat_ref.shape
    units, classes = w_two_ref.shape
    targets = spread.shape[0]
    chunk = targets // chunks
    span = key_s.shape[1]
    width_k = span // GROUP
    high = rows_dev // LOW
    started = []

    greet(all_steps)
    ids = page_ref[...]
    loose[0] = (ids // LOW).astype(jnp.float32).T
    loose[1] = (ids % LOW).astype(jnp.float32).T
    loose[2] = weight_ref[...].astype(jnp.float32).T
    count = ids.shape[1] // GROUP
    lists = [
        jnp.concatenate([loose[a, pl.ds(j, count, stride=GROUP), :] for j in range(GROUP)], axis=1)
        for a in range(3)
    ]
    pages_all[(0,) + tuple(place(s) for s in reversed(owner_steps))] = jnp.stack(lists).astype(jnp.bfloat16)
    stages = len(owner_steps)
    tiles = rows_dev // 512
    for k in range(stages - 1, -1, -1):
        flying = start_gather(owner_steps, k, 0, pages_all, page_sems[k], started)
        done = stages - 1 - k
        for i in range(done * tiles // stages, (done + 1) * tiles // stages):
            pre = dot(feat_ref[i * 512 : (i + 1) * 512, :], w_one_ref[...])
            active[i * 512 : (i + 1) * 512, :] = jnp.maximum(pre, 0.0).astype(jnp.bfloat16)
        settle(flying)

    lists = pages_all[0].astype(jnp.float32)
    lead = (slice(None),) * stages
    local = lists[lead + (0,)].reshape(-1, span) - (lax.axis_index(("own", "col")) * high).astype(jnp.float32)
    here = (local >= 0) & (local < high)
    lane_target = (lax.broadcasted_iota(jnp.int32, local.shape, 1) // width_k).astype(jnp.float32)
    key_s[...] = jnp.where(here, local * GROUP + lane_target, -1.0)
    low = lists[lead + (1,)].reshape(-1, span)
    for b in range(low_s.shape[0]):
        low_s[b] = low[b * 8 : (b + 1) * 8, :].T
    weight_s[...] = lists[lead + (2,)].reshape(-1, span)

    zero = jnp.zeros((), jnp.bfloat16)
    one = jnp.ones((), jnp.bfloat16)
    key_rows = lax.broadcasted_iota(jnp.int32, (high * GROUP, span), 0).astype(jnp.float32).astype(jnp.bfloat16)
    low_lanes = lax.broadcasted_iota(jnp.int32, (span, LOW), 1).astype(jnp.float32).astype(jnp.bfloat16)

    def build(i, carry):
        at = pl.ds(pl.multiple_of(i * 8, 8), 8)
        key = key_s[at, :].astype(jnp.bfloat16)
        low = low_s[i]
        weight = weight_s[at, :].astype(jnp.bfloat16)
        for pair in range(4):
            parts = []
            for g in (2 * pair, 2 * pair + 1):
                left = jnp.where(key_rows == key[g : g + 1, :], weight[g : g + 1, :], zero)
                column = jnp.broadcast_to(low[:, g : g + 1], (span, LOW)).astype(jnp.bfloat16)
                right = jnp.where(low_lanes == column, one, zero)
                parts.append(dot(left, right))
            rows = pl.ds(pl.multiple_of(i * 64 + pair * 16, 16), 16)
            for h in range(high):
                both = [p[h * GROUP : (h + 1) * GROUP, :] for p in parts]
                spread[rows, h * LOW : (h + 1) * LOW] = jnp.concatenate(both, axis=0).astype(jnp.bfloat16)
        return carry

    def sum_logits(c):
        for k, step in enumerate(inner):
            copies = start_scatter(step, c, held[k], recv[k], inner_sems[k], started)
            yield
            settle(copies)
            part = scatter_total(step, c, held[k], recv[k]).astype(jnp.bfloat16)
            if k + 1 < len(inner):
                held[k + 1][c] = part.reshape(held[k + 1].shape[1:])
            else:
                each = own[0][1] // chunks
                own_held[0, 0, c * each : (c + 1) * each] = part

    running = []
    blocks = chunk // 64
    for c in range(chunks):
        half = blocks // 2
        lax.fori_loop(c * blocks, c * blocks + half, build, 0)
        advance(running)
        lax.fori_loop(c * blocks + half, (c + 1) * blocks, build, 0)
        advance(running)
        block = dot(spread[c * chunk : (c + 1) * chunk, :], active[...]).astype(jnp.bfloat16)
        hidden[c * chunk : (c + 1) * chunk, :] = block
        held[0][c] = dot(block, w_two_ref[...]).astype(jnp.bfloat16).reshape(held[0].shape[1:])
        advance(running)
        running.append(sum_logits(c))
        next(running[-1])
    w_one_t = w_one_ref[...].T

    def transposed(first, last):
        for i in range(first * tiles // 8, last * tiles // 8):
            pre = dot_nt(w_one_t, feat_ref[i * 512 : (i + 1) * 512, :])
            active_t[:, i * 512 : (i + 1) * 512] = jnp.maximum(pre, 0.0).astype(jnp.bfloat16)

    transposed(0, 2)
    while running:
        advance(running)
    flying = start_scatter(own[0], 0, own_held, own_recv, own_sems, started)
    transposed(2, 5)
    settle(flying)
    logits = scatter_total(own[0], 0, own_held, own_recv)[0]
    rows = logits.shape[0]
    at_label = lax.broadcasted_iota(jnp.int32, (rows, label_ref.shape[1]), 0) + lax.axis_index("mlp") * rows
    lane = lax.broadcasted_iota(jnp.int32, at_label.shape, 1)
    label = jnp.sum(jnp.where(lane == at_label, label_ref[...].astype(jnp.float32), 0.0), axis=1, keepdims=True)
    exponent = jnp.exp(logits)
    category = lax.broadcasted_iota(jnp.int32, logits.shape, 1).astype(jnp.float32)
    probability = exponent / jnp.sum(exponent, axis=1, keepdims=True)
    d_logits = (probability - jnp.where(category == label, 1.0, 0.0)).astype(jnp.bfloat16)

    owner, upper, lower = place(own[0]), place(high_step), place(low_step)
    full[0, owner, upper, lower] = d_logits

    def send(where, sems, at, device):
        copy = pltpu.make_async_remote_copy(
            src_ref=full.at[where], dst_ref=full.at[where], send_sem=sems[0].at[at], recv_sem=sems[1].at[at],
            device_id=device, device_id_type=MESH)
        copy.start()
        started.append(copy)
        return copy

    members = own[0][1]
    landing = [
        send((0, owner, upper, lower), land_sems, (shift - 1,), partner(own[0], shift)[1])
        for shift in range(1, members)
    ]
    transposed(5, 7)
    crossing = []
    for shift in range(members):
        if shift:
            landing[shift - 1].wait_recv()
        origin = lax.rem(owner + members - shift, members)
        for hop in range(1, high_step[1]):
            crossing.append(send(
                (0, origin, upper, lower), cross_sems, (shift, hop - 1), partner(high_step, hop)[1]))
    other_core = partner(low_step, 1)[1]
    final = [send((0, slice(None), upper, lower), core_sems, (0,), other_core)]
    transposed(7, 8)
    settle(crossing)
    for hop in range(1, high_step[1]):
        origin = lax.rem(upper + high_step[1] - hop, high_step[1])
        final.append(send((0, slice(None), origin, lower), core_sems, (hop,), other_core))
    settle(final)
    d_logits = full[0].reshape(targets, classes)

    def sum_grads(p, values):
        grad_held[0][p] = values.astype(jnp.bfloat16).reshape(grad_held[0].shape[1:])
        count = len(grad_steps)
        for k, step in enumerate(grad_steps):
            copies = start_scatter(step, p, grad_held[k], grad_recv[k], scatter_sems[k], started)
            yield
            settle(copies)
            part = scatter_total(step, p, grad_held[k], grad_recv[k]).astype(jnp.bfloat16)
            if k + 1 < count:
                grad_held[k + 1][p] = part.reshape(grad_held[k + 1].shape[1:])
        grad_full[(p,) + tuple(place(s) for s in reversed(grad_steps))] = part[0]
        for k in range(count - 1, -1, -1):
            copies = start_gather(grad_steps, k, p, grad_full, gather_sems[k], started)
            yield
            settle(copies)
        block = grad_full[p].reshape(width_f, LANES).astype(jnp.float32)
        if p < units // LANES:
            one_ref[:, p * LANES : (p + 1) * LANES] = block
        else:
            q = p - units // LANES
            two_ref[:, q * LANES : (q + 1) * LANES] = block

    def launch(p, values):
        running.append(sum_grads(p, values))
        next(running[-1])

    d_logits_t = d_logits.T
    grad_two = dot(d_logits_t, hidden[...]).T
    for q in range(classes // LANES):
        launch(units // LANES + q, grad_two[:, q * LANES : (q + 1) * LANES])
    d_hidden[...] = dot(w_two_ref[...], d_logits_t).astype(jnp.bfloat16)
    part_units = 256
    width_r = 1024
    for u in range(units // part_units):
        rows = slice(u * part_units, (u + 1) * part_units)
        for r in range(rows_dev // width_r):
            at = slice(r * width_r, (r + 1) * width_r)
            spread_grad = dot(d_hidden[rows, :], spread[:, at])
            d_pre = jnp.where(active_t[rows, at] > 0, spread_grad, 0.0).astype(jnp.bfloat16)
            product = dot(d_pre, feat_ref[at, :])
            if r == 0:
                total[...] = product
            else:
                total[...] += product
            advance(running)
        for q in range(part_units // LANES):
            launch(u * (part_units // LANES) + q, total[q * LANES : (q + 1) * LANES, :].T)
    while running:
        advance(running)
    for copy in started:
        copy.wait_send()


def fused(nbr_page, nbr_weight, labels, features, w_one, w_two, owner_steps):
    inner = split_axis("mlp", (None,))
    own = [joined(owner_steps)]
    grad_steps = owner_steps
    all_steps = inner + own
    rows_dev, width_f = features.shape
    units, classes = w_two.shape
    lists, list_rows, span = 3, nbr_page.shape[0] // GROUP, GROUP * nbr_page.shape[1]
    sizes = lambda steps: [s[1] for s in steps]
    owners = 1
    for size in sizes(owner_steps):
        owners *= size
    groups = owners * list_rows
    targets = groups * GROUP
    chunks = lax.axis_size("own")
    bf16 = lambda *shape: pltpu.VMEM(shape, jnp.bfloat16)
    f32 = lambda *shape: pltpu.VMEM(shape, jnp.float32)

    def buffers(steps, pieces, outer, *block):
        held, recv = [], []
        for size in sizes(steps):
            outer //= size
            held.append(bf16(pieces, outer, size, *block))
            recv.append(bf16(pieces, size - 1, outer, *block))
        return held, recv

    own_rows = targets // owners
    for size in sizes(inner):
        own_rows //= size
    upper = lax.axis_size("mlp") // 2
    pieces = (units + classes) // LANES
    grad_rows = width_f // owners
    held, recv = buffers(inner, chunks, targets // chunks // own_rows, own_rows, classes)
    own_held, own_recv = buffers(own, 1, owners, own_rows, classes)
    grad_held, grad_recv = buffers(grad_steps, pieces, owners, grad_rows, LANES)

    def sems(steps, count):
        return [pltpu.SemaphoreType.DMA((count, s - 1)) for s in sizes(steps) for _ in range(2)]

    scratch = [
        f32(lists, *nbr_page.shape), bf16(1, *reversed(sizes(owner_steps)), lists, list_rows, span),
        f32(groups, span), f32(groups // 8, span, 8), f32(groups, span),
        bf16(rows_dev, units), bf16(units, rows_dev), bf16(targets, rows_dev), bf16(targets, units), bf16(units, targets),
        f32(256, width_f),
        *held, *recv, *own_held, *own_recv,
        bf16(1, owners, upper, 2, own_rows, classes),
        *grad_held, *grad_recv,
        bf16(pieces, *reversed(sizes(grad_steps)), grad_rows, LANES),
        *sems(owner_steps, 1), *sems(inner, chunks), *sems(own, 1),
        *[pltpu.SemaphoreType.DMA(shape) for shape in ((owners - 1,), (owners, upper - 1), (upper,)) for _ in range(2)],
        *sems(grad_steps, pieces), *sems(grad_steps, pieces),
    ]
    vmem = pl.BlockSpec(memory_space=pltpu.VMEM)
    return pl.pallas_call(
        functools.partial(fused_kernel, (inner, own, owner_steps, grad_steps)),
        in_specs=[vmem] * 6,
        out_specs=[vmem] * 2,
        out_shape=[
            jax.ShapeDtypeStruct((width_f, units), jnp.float32),
            jax.ShapeDtypeStruct((units, classes), jnp.float32),
        ],
        scratch_shapes=scratch,
        compiler_params=pltpu.CompilerParams(
            collective_id=3, has_side_effects=True, vmem_limit_bytes=VMEM_LIMIT),
    )(nbr_page.T, nbr_weight.T, labels.reshape(1, -1), features, w_one, w_two)


def body(features, nbr_page, nbr_weight, labels, w_one, w_two):
    own_axes = ("own", "col")
    units, classes = w_two.shape
    targets_dev, width_k = nbr_page.shape
    span = GROUP * width_k
    owner_steps = split_axis("col", (2, None)) + split_axis("own", (None,))
    all_steps = split_axis("mlp", (2, None)) + owner_steps
    owners = lax.axis_size(own_axes)
    small = targets_dev * owners * features.shape[0] <= SPREAD_LIMIT
    if small and owners * features.shape[0] <= LOW * LOW and lax.axis_size("mlp") >= 4:
        one, two = fused(nbr_page, nbr_weight, labels, features, w_one, w_two, owner_steps)
        return one, two
    pages, weights = gather_blocks(
        (nbr_page.reshape(-1, span), nbr_weight.reshape(-1, span)), owner_steps, 0)
    active_t, spread, hidden_t, part = forward(own_axes, pages, weights, features, w_one.T, w_two.T)
    dlog = sum_blocks(part, all_steps, 1, softmax_gradient, (labels[:, None],))
    grads = backward(dlog, hidden_t, w_two, spread, active_t, features)
    grads = sum_blocks(grads, owner_steps, 2).astype(jnp.float32)
    ones = units // LANES
    grad_one = jnp.concatenate([grads[p] for p in range(ones)], axis=1)
    grad_two = jnp.concatenate([grads[p] for p in range(ones, grads.shape[0])], axis=1)
    return grad_one, grad_two


def solution(mesh):
    placed = (
        P(("own", "col"), None),
        P(("own", "col"), None),
        P(("own", "col"), None),
        P(("own", "col")),
        P(None, "mlp"),
        P("mlp", None),
    )
    return jax.shard_map(
        body,
        mesh=mesh,
        in_specs=placed,
        out_specs=(P(None, "mlp"), P("mlp", None)),
        check_vma=False,
    )
```

```python
import functools
import jax
import jax.numpy as jnp
from jax import lax
from jax.experimental import pallas as pl
from jax.experimental.pallas import tpu as pltpu
from jax.sharding import PartitionSpec as P

GROUP = 8
LOW = 256
LANES = 128
SPREAD_LIMIT = 8 * 1024 * 1024
NT = (((1,), (1,)), ((), ()))
VMEM_LIMIT = 56 * 1024 * 1024


def dot(a, b):
    return jnp.dot(a, b, preferred_element_type=jnp.float32)


def dot_nt(a, b):
    return lax.dot_general(a, b, NT, preferred_element_type=jnp.float32)


MESH = pl.DeviceIdType.MESH


def split_axis(axis, parts):
    size = lax.axis_size(axis)
    steps, stride = [], 1
    for members in parts:
        members = size // stride if members is None else min(members, size // stride)
        if members > 1:
            steps.append((axis, members, stride))
        stride *= members
    return steps


def joined(steps):
    members = 1
    for step in steps:
        members *= step[1]
    return (tuple(steps), members, 0)


def place(step):
    axis, members, stride = step
    if stride:
        return lax.rem(lax.div(lax.axis_index(axis), stride), members)
    mine, weight = 0, 1
    for part in axis:
        mine = mine + place(part) * weight
        weight *= part[1]
    return mine


def partner(step, shift):
    axis, members, stride = step
    mine = place(step)
    other = lax.rem(mine + shift, members)
    if stride:
        return other, {axis: lax.axis_index(axis) + (other - mine) * stride}
    device, rest = {}, other
    for part in axis:
        device[part[0]] = lax.axis_index(part[0]) + (lax.rem(rest, part[1]) - place(part)) * part[2]
        rest = lax.div(rest, part[1])
    return other, device


def greet(steps):
    barrier = pltpu.get_barrier_semaphore()
    count = 0
    for step in steps:
        for shift in range(1, step[1]):
            pl.semaphore_signal(barrier, inc=1, device_id=partner(step, shift)[1], device_id_type=MESH)
            count += 1
    pl.semaphore_wait(barrier, count)


def start_scatter(step, piece, held, recv, sems, started):
    copies = []
    for shift in range(1, step[1]):
        other, device = partner(step, shift)
        copy = pltpu.make_async_remote_copy(
            src_ref=held.at[piece, :, other], dst_ref=recv.at[piece, shift - 1],
            send_sem=sems[0].at[piece, shift - 1], recv_sem=sems[1].at[piece, shift - 1],
            device_id=device, device_id_type=MESH)
        copy.start()
        copies.append(copy)
    started.extend(copies)
    return copies


def start_gather(steps, k, piece, full, sems, started):
    where = (piece,) + (slice(None),) * (len(steps) - 1 - k) + tuple(place(s) for s in reversed(steps[: k + 1]))
    copies = []
    for shift in range(1, steps[k][1]):
        copy = pltpu.make_async_remote_copy(
            src_ref=full.at[where], dst_ref=full.at[where],
            send_sem=sems[0].at[piece, shift - 1], recv_sem=sems[1].at[piece, shift - 1],
            device_id=partner(steps[k], shift)[1], device_id_type=MESH)
        copy.start()
        copies.append(copy)
    started.extend(copies)
    return copies


def settle(copies):
    for copy in copies:
        copy.wait_recv()


def sum_kernel(steps, pieces, finish, n_extra, *refs):
    first = refs[0]
    extra = refs[1 : 1 + n_extra]
    full = refs[1 + n_extra]
    scratch = refs[2 + n_extra :]
    count = len(steps)
    recv, held = scratch[:count], (first,) + scratch[count : 2 * count - 1]
    sems = scratch[2 * count - 1 :]
    scatter_sems = [(sems[2 * k], sems[2 * k + 1]) for k in range(count)]
    gather_sems = [(sems[2 * (count + k)], sems[2 * (count + k) + 1]) for k in range(count)]
    greet(steps)
    started = []
    flying = [start_scatter(steps[0], p, held[0], recv[0], scatter_sems[0], started) for p in range(pieces)]
    last = []
    for k in range(count):
        following = []
        for p in range(pieces):
            settle(flying[p])
            total = held[k][p, :, place(steps[k])].astype(jnp.float32)
            for j in range(steps[k][1] - 1):
                total = total + recv[k][p, j].astype(jnp.float32)
            if k + 1 < count:
                held[k + 1][p] = total.astype(jnp.bfloat16).reshape(held[k + 1].shape[1:])
                following.append(start_scatter(steps[k + 1], p, held[k + 1], recv[k + 1], scatter_sems[k + 1], started))
            else:
                last.append(total.reshape(total.shape[1:]))
                if finish is None:
                    full[(p,) + tuple(place(s) for s in reversed(steps))] = last[p].astype(jnp.bfloat16)
                    following.append(start_gather(steps, k, p, full, gather_sems[k], started))
        flying = following
    if finish is not None:
        results = finish(last, *extra)
        for p in range(pieces):
            full[(p,) + tuple(place(s) for s in reversed(steps))] = results[p].astype(jnp.bfloat16)
            flying.append(start_gather(steps, count - 1, p, full, gather_sems[count - 1], started))
    for k in range(count - 2, -1, -1):
        following = []
        for p in range(pieces):
            settle(flying[p])
            following.append(start_gather(steps, k, p, full, gather_sems[k], started))
        flying = following
    for p in range(pieces):
        settle(flying[p])
    for copy in started:
        copy.wait_send()


def sum_blocks(array, steps, collective_id, finish=None, extra=()):
    pieces, rows, lanes = array.shape
    sizes = [s[1] for s in steps]
    block = rows
    for size in sizes:
        block //= size
    recv, held, outer = [], [], rows // block
    for k, size in enumerate(sizes):
        outer //= size
        if k == 0:
            first = array.reshape(pieces, outer, size, block, lanes)
        else:
            held.append(pltpu.VMEM((pieces, outer, size, block, lanes), jnp.bfloat16))
        recv.append(pltpu.VMEM((pieces, size - 1, outer, block, lanes), jnp.bfloat16))
    sems = [pltpu.SemaphoreType.DMA((pieces, size - 1)) for size in sizes for _ in range(2)] * 2
    vmem = pl.BlockSpec(memory_space=pltpu.VMEM)
    full = pl.pallas_call(
        functools.partial(sum_kernel, steps, pieces, finish, len(extra)),
        in_specs=[vmem] * (1 + len(extra)),
        out_specs=vmem,
        out_shape=jax.ShapeDtypeStruct((pieces, *reversed(sizes), block, lanes), jnp.bfloat16),
        scratch_shapes=recv + held + sems,
        compiler_params=pltpu.CompilerParams(
            collective_id=collective_id, has_side_effects=True, vmem_limit_bytes=VMEM_LIMIT),
    )(first, *extra)
    return full.reshape(pieces, rows, lanes)


def gather_kernel(steps, *refs):
    count = len(refs) // 3
    ins, outs, sems = refs[:count], refs[count : 2 * count], refs[2 * count :]
    where = (0,) + tuple(place(s) for s in reversed(steps))
    greet(steps)
    started = []
    for a in range(count):
        outs[a][where] = ins[a][...]
    for k in range(len(steps) - 1, -1, -1):
        flying = []
        for a in range(count):
            pair = (sems[a].at[k, 0], sems[a].at[k, 1])
            flying.extend(start_gather(steps, k, 0, outs[a], pair, started))
        settle(flying)
    for copy in started:
        copy.wait_send()


def gather_blocks(arrays, steps, collective_id):
    sizes = [s[1] for s in steps]
    vmem = pl.BlockSpec(memory_space=pltpu.VMEM)
    outs = pl.pallas_call(
        functools.partial(gather_kernel, steps),
        in_specs=[vmem] * len(arrays),
        out_specs=[vmem] * len(arrays),
        out_shape=[jax.ShapeDtypeStruct((1, *reversed(sizes), *a.shape), a.dtype) for a in arrays],
        scratch_shapes=[pltpu.SemaphoreType.DMA((len(steps), 2, 1, max(sizes) - 1))] * len(arrays),
        compiler_params=pltpu.CompilerParams(
            collective_id=collective_id, has_side_effects=True, vmem_limit_bytes=VMEM_LIMIT),
    )(*arrays)
    return [o.reshape(-1, o.shape[-1]) for o in outs]


def softmax_gradient(logits, label_ref):
    lanes = logits[0].shape[1]
    rows = logits[0].shape[0]
    start = pl.multiple_of(lax.axis_index("mlp") * rows, rows)
    label = label_ref[pl.ds(start, rows), :]
    exponent = [jnp.exp(x) for x in logits]
    total = sum(jnp.sum(e, axis=1, keepdims=True) for e in exponent)
    results = []
    for p, e in enumerate(exponent):
        category = lax.broadcasted_iota(jnp.int32, e.shape, 1) + p * lanes
        results.append(e / total - jnp.where(category == label, 1.0, 0.0))
    return results


def build_spread(page_ref, weight_ref, first_row, rows_dev, spread_ref, chunk):
    span = page_ref.shape[1]
    width_k = span // GROUP
    high = rows_dev // LOW
    local = page_ref[...] - first_row
    here = (local >= 0) & (local < rows_dev)
    lane_target = lax.broadcasted_iota(jnp.int32, local.shape, 1) // width_k
    key = jnp.where(here, (local // LOW) * GROUP + lane_target, -1).astype(jnp.float32)
    low = jnp.where(here, local % LOW, -1).astype(jnp.float32)
    key = key.astype(jnp.bfloat16)
    low = low.astype(jnp.bfloat16)
    weight = weight_ref[...]
    zero = jnp.zeros((), jnp.bfloat16)
    one = jnp.ones((), jnp.bfloat16)
    key_rows = lax.broadcasted_iota(jnp.int32, (high * GROUP, span), 0).astype(jnp.float32).astype(jnp.bfloat16)
    low_rows = lax.broadcasted_iota(jnp.int32, (LOW, span), 0).astype(jnp.float32).astype(jnp.bfloat16)
    for pair in range(chunk // (2 * GROUP)):
        parts = []
        for g in (2 * pair, 2 * pair + 1):
            left = jnp.where(key_rows == key[g : g + 1, :], weight[g : g + 1, :], zero)
            right = jnp.where(low_rows == low[g : g + 1, :], one, zero)
            parts.append(dot_nt(left, right))
        for h in range(high):
            rows = [p[h * GROUP : (h + 1) * GROUP, :] for p in parts]
            spread_ref[2 * GROUP * pair : 2 * GROUP * (pair + 1), h * LOW : (h + 1) * LOW] = (
                jnp.concatenate(rows, axis=0).astype(jnp.bfloat16)
            )


def forward_kernel(own_axes, page_ref, weight_ref, feat_ref, w_one_t_ref, w_two_t_ref,
                   active_ref, spread_ref, hidden_ref, logit_ref):
    rows_dev = feat_ref.shape[0]
    chunk = spread_ref.shape[0]
    first_row = lax.axis_index(own_axes) * rows_dev

    @pl.when(pl.program_id(0) == 0)
    def _():
        def tile(i, _):
            at = pl.ds(pl.multiple_of(i * 512, 512), 512)
            pre = dot_nt(w_one_t_ref[...], feat_ref[at, :])
            active_ref[:, at] = jnp.maximum(pre, 0.0).astype(jnp.bfloat16)
            return 0
        lax.fori_loop(0, rows_dev // 512, tile, 0)

    build_spread(page_ref, weight_ref, first_row, rows_dev, spread_ref, chunk)
    hidden = dot_nt(active_ref[...], spread_ref[...]).astype(jnp.bfloat16)
    hidden_ref[...] = hidden
    logits = dot(w_two_t_ref[...], hidden).T.astype(jnp.bfloat16)
    lanes = logit_ref.shape[2]
    for p in range(logit_ref.shape[0]):
        logit_ref[p] = logits[:, p * lanes : (p + 1) * lanes]


def forward(own_axes, pages, weights, features, w_one_t, w_two_t):
    rows_dev, width_f = features.shape
    units = w_one_t.shape[0]
    classes = w_two_t.shape[0]
    groups, span = pages.shape
    targets = groups * GROUP
    chunk = min(256, targets)
    steps = targets // chunk
    whole = lambda shape: pl.BlockSpec(shape, lambda i: (0, 0))
    return pl.pallas_call(
        functools.partial(forward_kernel, own_axes),
        grid=(steps,),
        in_specs=[
            pl.BlockSpec((chunk // GROUP, span), lambda i: (i, 0)),
            pl.BlockSpec((chunk // GROUP, span), lambda i: (i, 0)),
            whole((rows_dev, width_f)),
            whole((units, width_f)),
            whole((classes, units)),
        ],
        out_specs=[
            whole((units, rows_dev)),
            pl.BlockSpec((chunk, rows_dev), lambda i: (i, 0)),
            pl.BlockSpec((units, chunk), lambda i: (0, i)),
            pl.BlockSpec((classes // LANES, chunk, LANES), lambda i: (0, i, 0)),
        ],
        out_shape=[
            jax.ShapeDtypeStruct((units, rows_dev), jnp.bfloat16),
            jax.ShapeDtypeStruct((targets, rows_dev), jnp.bfloat16),
            jax.ShapeDtypeStruct((units, targets), jnp.bfloat16),
            jax.ShapeDtypeStruct((classes // LANES, targets, LANES), jnp.bfloat16),
        ],
        compiler_params=pltpu.CompilerParams(vmem_limit_bytes=VMEM_LIMIT),
    )(pages, weights, features, w_one_t, w_two_t)


def backward_kernel(dlog_ref, hidden_ref, w_two_ref, spread_ref, active_ref, feat_ref,
                    grad_ref, d_hidden, total):
    step = pl.program_id(0)
    units = total.shape[0]
    width_f = total.shape[1]
    ones = units // LANES

    @pl.when(step == 0)
    def _():
        d_logits = jnp.concatenate([dlog_ref[p] for p in range(dlog_ref.shape[0])], axis=1)
        d_hidden[...] = dot_nt(w_two_ref[...], d_logits).astype(jnp.bfloat16)
        grad_two = dot(hidden_ref[...], d_logits).astype(jnp.bfloat16)
        for p in range(grad_two.shape[1] // LANES):
            grad_ref[ones + p] = grad_two[:, p * LANES : (p + 1) * LANES]
        total[...] = jnp.zeros_like(total)

    spread_grad = dot(d_hidden[...], spread_ref[...])
    d_pre = jnp.where(active_ref[...] > 0, spread_grad, 0.0).astype(jnp.bfloat16)
    total[...] += dot(d_pre, feat_ref[...])

    @pl.when(step == pl.num_programs(0) - 1)
    def _():
        for p in range(ones):
            grad_ref[p] = total[p * LANES : (p + 1) * LANES, :].T.astype(jnp.bfloat16)


def backward(dlog, hidden_t, w_two, spread, active_t, features):
    rows_dev, width_f = features.shape
    units, classes = w_two.shape
    assert units == width_f
    targets = spread.shape[0]
    block = 512
    whole = lambda shape: pl.BlockSpec(shape, lambda i: (0,) * len(shape))
    out = ((units + classes) // LANES, width_f, LANES)
    return pl.pallas_call(
        backward_kernel,
        grid=(rows_dev // block,),
        in_specs=[
            whole(dlog.shape),
            whole((units, targets)),
            whole((units, classes)),
            pl.BlockSpec((targets, block), lambda i: (0, i)),
            pl.BlockSpec((units, block), lambda i: (0, i)),
            pl.BlockSpec((block, width_f), lambda i: (i, 0)),
        ],
        out_specs=whole(out),
        out_shape=jax.ShapeDtypeStruct(out, jnp.bfloat16),
        scratch_shapes=[
            pltpu.VMEM((units, targets), jnp.bfloat16),
            pltpu.VMEM((units, width_f), jnp.float32),
        ],
        compiler_params=pltpu.CompilerParams(vmem_limit_bytes=VMEM_LIMIT),
    )(dlog, hidden_t, w_two, spread, active_t, features)


def scatter_total(step, piece, held, recv):
    total = held[piece, :, place(step)].astype(jnp.float32)
    for j in range(step[1] - 1):
        total = total + recv[piece, j].astype(jnp.float32)
    return total


def advance(running):
    for task in list(running):
        if next(task, "done") == "done":
            running.remove(task)


def fused_kernel(plan, *refs):
    it = iter(refs)
    page_ref, weight_ref, label_ref, feat_hbm, w_one_ref, w_two_ref, one_ref, two_ref = (next(it) for _ in range(8))
    feat_ref, feat_sem = next(it), next(it)
    loose, pages_all, key_s, low_s, weight_s, active, active_t, spread, hidden, d_hidden, total = (next(it) for _ in range(11))
    inner, own, owner_steps, grad_steps = plan
    all_steps = inner + own
    low_step, high_step = split_axis("mlp", (2, None))
    chunks = lax.axis_size("own")
    held = [next(it) for _ in inner]
    recv = [next(it) for _ in inner]
    own_held, own_recv, full = (next(it) for _ in range(3))
    grad_held = [next(it) for _ in grad_steps]
    grad_recv = [next(it) for _ in grad_steps]
    grad_full = next(it)
    pairs = lambda n: [(next(it), next(it)) for _ in range(n)]
    page_sems = pairs(len(owner_steps))
    inner_sems = pairs(len(inner))
    own_sems = pairs(1)[0]
    land_sems, cross_sems, core_sems = pairs(3)
    scatter_sems = pairs(len(grad_steps))
    gather_sems = pairs(len(grad_steps))

    rows_dev, width_f = feat_ref.shape
    units, classes = w_two_ref.shape
    targets = spread.shape[0]
    chunk = targets // chunks
    span = key_s.shape[1]
    width_k = span // GROUP
    high = rows_dev // LOW
    started = []

    load = pltpu.make_async_copy(feat_hbm, feat_ref, feat_sem)
    load.start()
    greet(all_steps)
    ids = page_ref[...]
    loose[0] = (ids // LOW).astype(jnp.float32).T
    loose[1] = (ids % LOW).astype(jnp.float32).T
    loose[2] = weight_ref[...].astype(jnp.float32).T
    count = ids.shape[1] // GROUP
    lists = [
        jnp.concatenate([loose[a, pl.ds(j, count, stride=GROUP), :] for j in range(GROUP)], axis=1)
        for a in range(3)
    ]
    pages_all[(0,) + tuple(place(s) for s in reversed(owner_steps))] = jnp.stack(lists).astype(jnp.bfloat16)
    stages = len(owner_steps)
    tiles = rows_dev // 512
    for k in range(stages - 1, -1, -1):
        flying = start_gather(owner_steps, k, 0, pages_all, page_sems[k], started)
        done = stages - 1 - k
        if done == 0:
            load.wait()
        for i in range(done * tiles // stages, (done + 1) * tiles // stages):
            pre = dot(feat_ref[i * 512 : (i + 1) * 512, :], w_one_ref[...])
            active[i * 512 : (i + 1) * 512, :] = jnp.maximum(pre, 0.0).astype(jnp.bfloat16)
        settle(flying)

    lists = pages_all[0].astype(jnp.float32)
    lead = (slice(None),) * stages
    local = lists[lead + (0,)].reshape(-1, span) - (lax.axis_index(("own", "col")) * high).astype(jnp.float32)
    here = (local >= 0) & (local < high)
    lane_target = (lax.broadcasted_iota(jnp.int32, local.shape, 1) // width_k).astype(jnp.float32)
    key_s[...] = jnp.where(here, local * GROUP + lane_target, -1.0)
    low = lists[lead + (1,)].reshape(-1, span)
    for b in range(low_s.shape[0]):
        low_s[b] = low[b * 8 : (b + 1) * 8, :].T
    weight_s[...] = lists[lead + (2,)].reshape(-1, span)

    zero = jnp.zeros((), jnp.bfloat16)
    one = jnp.ones((), jnp.bfloat16)
    key_rows = lax.broadcasted_iota(jnp.int32, (high * GROUP, span), 0).astype(jnp.float32).astype(jnp.bfloat16)
    low_lanes = lax.broadcasted_iota(jnp.int32, (span, LOW), 1).astype(jnp.float32).astype(jnp.bfloat16)

    def build(i, carry):
        at = pl.ds(pl.multiple_of(i * 8, 8), 8)
        key = key_s[at, :].astype(jnp.bfloat16)
        low = low_s[i]
        weight = weight_s[at, :].astype(jnp.bfloat16)
        for pair in range(4):
            parts = []
            for g in (2 * pair, 2 * pair + 1):
                left = jnp.where(key_rows == key[g : g + 1, :], weight[g : g + 1, :], zero)
                column = jnp.broadcast_to(low[:, g : g + 1], (span, LOW)).astype(jnp.bfloat16)
                right = jnp.where(low_lanes == column, one, zero)
                parts.append(dot(left, right))
            rows = pl.ds(pl.multiple_of(i * 64 + pair * 16, 16), 16)
            for h in range(high):
                both = [p[h * GROUP : (h + 1) * GROUP, :] for p in parts]
                spread[rows, h * LOW : (h + 1) * LOW] = jnp.concatenate(both, axis=0).astype(jnp.bfloat16)
        return carry

    def sum_logits(c):
        for k, step in enumerate(inner):
            copies = start_scatter(step, c, held[k], recv[k], inner_sems[k], started)
            yield
            settle(copies)
            part = scatter_total(step, c, held[k], recv[k]).astype(jnp.bfloat16)
            if k + 1 < len(inner):
                held[k + 1][c] = part.reshape(held[k + 1].shape[1:])
            else:
                each = own[0][1] // chunks
                own_held[0, 0, c * each : (c + 1) * each] = part

    running = []
    blocks = chunk // 64
    for c in range(chunks):
        half = blocks // 2
        lax.fori_loop(c * blocks, c * blocks + half, build, 0)
        advance(running)
        lax.fori_loop(c * blocks + half, (c + 1) * blocks, build, 0)
        advance(running)
        block = dot(spread[c * chunk : (c + 1) * chunk, :], active[...]).astype(jnp.bfloat16)
        hidden[c * chunk : (c + 1) * chunk, :] = block
        held[0][c] = dot(block, w_two_ref[...]).astype(jnp.bfloat16).reshape(held[0].shape[1:])
        advance(running)
        running.append(sum_logits(c))
        next(running[-1])
    w_one_t = w_one_ref[...].T

    def transposed(first, last):
        for i in range(first * tiles // 8, last * tiles // 8):
            pre = dot_nt(w_one_t, feat_ref[i * 512 : (i + 1) * 512, :])
            active_t[:, i * 512 : (i + 1) * 512] = jnp.maximum(pre, 0.0).astype(jnp.bfloat16)

    transposed(0, 2)
    while running:
        advance(running)
    flying = start_scatter(own[0], 0, own_held, own_recv, own_sems, started)
    transposed(2, 5)
    settle(flying)
    logits = scatter_total(own[0], 0, own_held, own_recv)[0]
    rows = logits.shape[0]
    at_label = lax.broadcasted_iota(jnp.int32, (rows, label_ref.shape[1]), 0) + lax.axis_index("mlp") * rows
    lane = lax.broadcasted_iota(jnp.int32, at_label.shape, 1)
    label = jnp.sum(jnp.where(lane == at_label, label_ref[...].astype(jnp.float32), 0.0), axis=1, keepdims=True)
    exponent = jnp.exp(logits)
    category = lax.broadcasted_iota(jnp.int32, logits.shape, 1).astype(jnp.float32)
    probability = exponent / jnp.sum(exponent, axis=1, keepdims=True)
    d_logits = (probability - jnp.where(category == label, 1.0, 0.0)).astype(jnp.bfloat16)

    owner, upper, lower = place(own[0]), place(high_step), place(low_step)
    full[0, owner, upper, lower] = d_logits

    def send(where, sems, at, device):
        copy = pltpu.make_async_remote_copy(
            src_ref=full.at[where], dst_ref=full.at[where], send_sem=sems[0].at[at], recv_sem=sems[1].at[at],
            device_id=device, device_id_type=MESH)
        copy.start()
        started.append(copy)
        return copy

    members = own[0][1]
    landing = [
        send((0, owner, upper, lower), land_sems, (shift - 1,), partner(own[0], shift)[1])
        for shift in range(1, members)
    ]
    transposed(5, 7)
    crossing = []
    for shift in range(members):
        if shift:
            landing[shift - 1].wait_recv()
        origin = lax.rem(owner + members - shift, members)
        for hop in range(1, high_step[1]):
            crossing.append(send(
                (0, origin, upper, lower), cross_sems, (shift, hop - 1), partner(high_step, hop)[1]))
    other_core = partner(low_step, 1)[1]
    final = [send((0, slice(None), upper, lower), core_sems, (0,), other_core)]
    transposed(7, 8)
    settle(crossing)
    for hop in range(1, high_step[1]):
        origin = lax.rem(upper + high_step[1] - hop, high_step[1])
        final.append(send((0, slice(None), origin, lower), core_sems, (hop,), other_core))
    settle(final)
    d_logits = full[0].reshape(targets, classes)

    def sum_grads(p, values):
        grad_held[0][p] = values.astype(jnp.bfloat16).reshape(grad_held[0].shape[1:])
        count = len(grad_steps)
        for k, step in enumerate(grad_steps):
            copies = start_scatter(step, p, grad_held[k], grad_recv[k], scatter_sems[k], started)
            yield
            settle(copies)
            part = scatter_total(step, p, grad_held[k], grad_recv[k]).astype(jnp.bfloat16)
            if k + 1 < count:
                grad_held[k + 1][p] = part.reshape(grad_held[k + 1].shape[1:])
        grad_full[(p,) + tuple(place(s) for s in reversed(grad_steps))] = part[0]
        for k in range(count - 1, -1, -1):
            copies = start_gather(grad_steps, k, p, grad_full, gather_sems[k], started)
            yield
            settle(copies)
        block = grad_full[p].reshape(width_f, LANES)
        if p < units // LANES:
            one_ref[:, p * LANES : (p + 1) * LANES] = block
        else:
            q = p - units // LANES
            two_ref[:, q * LANES : (q + 1) * LANES] = block

    def launch(p, values):
        running.append(sum_grads(p, values))
        next(running[-1])

    d_logits_t = d_logits.T
    grad_two = dot(d_logits_t, hidden[...]).T
    for q in range(classes // LANES):
        launch(units // LANES + q, grad_two[:, q * LANES : (q + 1) * LANES])
    d_hidden[...] = dot(w_two_ref[...], d_logits_t).astype(jnp.bfloat16)
    part_units = 256
    width_r = 1024
    for u in range(units // part_units):
        rows = slice(u * part_units, (u + 1) * part_units)
        for r in range(rows_dev // width_r):
            at = slice(r * width_r, (r + 1) * width_r)
            spread_grad = dot(d_hidden[rows, :], spread[:, at])
            d_pre = jnp.where(active_t[rows, at] > 0, spread_grad, 0.0).astype(jnp.bfloat16)
            product = dot(d_pre, feat_ref[at, :])
            if r == 0:
                total[...] = product
            else:
                total[...] += product
            if r % 2 == 1:
                advance(running)
        for q in range(part_units // LANES):
            launch(u * (part_units // LANES) + q, total[q * LANES : (q + 1) * LANES, :].T)
    while running:
        advance(running)
    for copy in started:
        copy.wait_send()


def fused(nbr_page, nbr_weight, labels, features, w_one, w_two, owner_steps):
    inner = split_axis("mlp", (None,))
    own = [joined(owner_steps)]
    grad_steps = owner_steps
    all_steps = inner + own
    rows_dev, width_f = features.shape
    units, classes = w_two.shape
    lists, list_rows, span = 3, nbr_page.shape[0] // GROUP, GROUP * nbr_page.shape[1]
    sizes = lambda steps: [s[1] for s in steps]
    owners = 1
    for size in sizes(owner_steps):
        owners *= size
    groups = owners * list_rows
    targets = groups * GROUP
    chunks = lax.axis_size("own")
    bf16 = lambda *shape: pltpu.VMEM(shape, jnp.bfloat16)
    f32 = lambda *shape: pltpu.VMEM(shape, jnp.float32)

    def buffers(steps, pieces, outer, *block):
        held, recv = [], []
        for size in sizes(steps):
            outer //= size
            held.append(bf16(pieces, outer, size, *block))
            recv.append(bf16(pieces, size - 1, outer, *block))
        return held, recv

    own_rows = targets // owners
    for size in sizes(inner):
        own_rows //= size
    upper = lax.axis_size("mlp") // 2
    pieces = (units + classes) // LANES
    grad_rows = width_f // owners
    held, recv = buffers(inner, chunks, targets // chunks // own_rows, own_rows, classes)
    own_held, own_recv = buffers(own, 1, owners, own_rows, classes)
    grad_held, grad_recv = buffers(grad_steps, pieces, owners, grad_rows, LANES)

    def sems(steps, count):
        return [pltpu.SemaphoreType.DMA((count, s - 1)) for s in sizes(steps) for _ in range(2)]

    scratch = [
        bf16(rows_dev, width_f), pltpu.SemaphoreType.DMA, f32(lists, *nbr_page.shape), bf16(1, *reversed(sizes(owner_steps)), lists, list_rows, span),
        f32(groups, span), f32(groups // 8, span, 8), f32(groups, span),
        bf16(rows_dev, units), bf16(units, rows_dev), bf16(targets, rows_dev), bf16(targets, units), bf16(units, targets),
        f32(256, width_f),
        *held, *recv, *own_held, *own_recv,
        bf16(1, owners, upper, 2, own_rows, classes),
        *grad_held, *grad_recv,
        bf16(pieces, *reversed(sizes(grad_steps)), grad_rows, LANES),
        *sems(owner_steps, 1), *sems(inner, chunks), *sems(own, 1),
        *[pltpu.SemaphoreType.DMA(shape) for shape in ((owners - 1,), (owners, upper - 1), (upper,)) for _ in range(2)],
        *sems(grad_steps, pieces), *sems(grad_steps, pieces),
    ]
    vmem = pl.BlockSpec(memory_space=pltpu.VMEM)
    return pl.pallas_call(
        functools.partial(fused_kernel, (inner, own, owner_steps, grad_steps)),
        in_specs=[vmem] * 3 + [pl.BlockSpec(memory_space=pl.ANY)] + [vmem] * 2,
        out_specs=[vmem] * 2,
        out_shape=[
            jax.ShapeDtypeStruct((width_f, units), jnp.bfloat16),
            jax.ShapeDtypeStruct((units, classes), jnp.bfloat16),
        ],
        scratch_shapes=scratch,
        compiler_params=pltpu.CompilerParams(
            collective_id=3, has_side_effects=True, vmem_limit_bytes=VMEM_LIMIT),
    )(nbr_page.T, nbr_weight.T, labels.reshape(1, -1), features, w_one, w_two)


def widen_kernel(one_ref, two_ref, one_out, two_out):
    one_out[...] = one_ref[...].astype(jnp.float32)
    two_out[...] = two_ref[...].astype(jnp.float32)


def widen(one, two):
    vmem = pl.BlockSpec(memory_space=pltpu.VMEM)
    return pl.pallas_call(
        widen_kernel,
        in_specs=[vmem] * 2,
        out_specs=[vmem] * 2,
        out_shape=[jax.ShapeDtypeStruct(a.shape, jnp.float32) for a in (one, two)],
        compiler_params=pltpu.CompilerParams(vmem_limit_bytes=VMEM_LIMIT),
    )(one, two)


def body(features, nbr_page, nbr_weight, labels, w_one, w_two):
    own_axes = ("own", "col")
    units, classes = w_two.shape
    targets_dev, width_k = nbr_page.shape
    span = GROUP * width_k
    owner_steps = split_axis("col", (2, None)) + split_axis("own", (None,))
    all_steps = split_axis("mlp", (2, None)) + owner_steps
    owners = lax.axis_size(own_axes)
    small = targets_dev * owners * features.shape[0] <= SPREAD_LIMIT
    if small and owners * features.shape[0] <= LOW * LOW and lax.axis_size("mlp") >= 4:
        one, two = fused(nbr_page, nbr_weight, labels, features, w_one, w_two, owner_steps)
        return widen(one, two)
    pages, weights = gather_blocks(
        (nbr_page.reshape(-1, span), nbr_weight.reshape(-1, span)), owner_steps, 0)
    active_t, spread, hidden_t, part = forward(own_axes, pages, weights, features, w_one.T, w_two.T)
    dlog = sum_blocks(part, all_steps, 1, softmax_gradient, (labels[:, None],))
    grads = backward(dlog, hidden_t, w_two, spread, active_t, features)
    grads = sum_blocks(grads, owner_steps, 2).astype(jnp.float32)
    ones = units // LANES
    grad_one = jnp.concatenate([grads[p] for p in range(ones)], axis=1)
    grad_two = jnp.concatenate([grads[p] for p in range(ones, grads.shape[0])], axis=1)
    return grad_one, grad_two


def solution(mesh):
    placed = (
        P(("own", "col"), None),
        P(("own", "col"), None),
        P(("own", "col"), None),
        P(("own", "col")),
        P(None, "mlp"),
        P("mlp", None),
    )
    return jax.shard_map(
        body,
        mesh=mesh,
        in_specs=placed,
        out_specs=(P(None, "mlp"), P("mlp", None)),
        check_vma=False,
    )
```
